256 devices in a mesh: section: 16 (over z_hi, y), dp: 16 (over z_lo, x, core).
Axes of the slice: x: 4, y: 4, z: 8 (z_hi: 4, z_lo: 2; z = z_hi * 2 + z_lo), core: 2. Of those that a mesh axis runs over, the one named last changes fastest.
Arguments:
- inputs: bfloat16 [4096, 1024], P('dp'), may hold values from -6 to 6
- segment_ids: int32 [64, 64], P('dp'), may hold values from 0 to 3, never falling along the last dimension, each value on 1 to 32 neighbouring positions
- cotangent: bfloat16 [4096, 1024], P('dp'), may hold values from -0.125 to 0.125
- gains: bfloat16 [16, 1024], P('section'), may hold values from 0.5 to 1.5
- w_qkv: bfloat16 [16, 1024, 1536], P('section', 'dp'), may hold values from -0.1875 to 0.1875
- w_out: bfloat16 [16, 512, 1024], P('section', 'dp'), may hold values from -0.25 to 0.25
Outputs:
- grad_qkv: float32 [16, 1024, 1536], P('section', 'dp')
- grad_out: float32 [16, 512, 1024], P('section', 'dp')
- grad_gain: float32 [16, 1024], P('section', 'dp')
The draws below stay inside these ranges and needn't reach their ends.
Inputs may be any that keep to these rules, and one draw needn't show every extreme that they name: `segment_ids`: within each sequence the ids never fall; each document holds 1 to 32 tokens.
All inputs are finite; a program needn't handle non-finite values.
Results may differ from the reference program's by a relative error of at most 0.04.
Values may be sent and summed in bfloat16 or wider, within the bound.
No kernel may reach another device: no remote copies, remote signals or barrier semaphores. Data moves between devices by JAX's collectives and lax.ppermute only.
A program may use at most 128 MiB of HBM per device.

```python
import math
import jax
import jax.numpy as jnp
import numpy as np
from jax import lax

D = 1024
HEADS = 8
HEAD_DIM = 64
SEQ = 64
MICRO = 2
DOCS = 4
DOC_MOST = 32
ATTN_WIDTH = 512
LAYERS = 16
SEQS = 64
TOKENS = 4096


def block_levels(key, shape, cuts, least, largest):
    def one(axis_at, blocks):
        heights = jax.random.uniform(jax.random.fold_in(jax.random.fold_in(key, 6), axis_at), (blocks,), jnp.float32, least / len(cuts), largest / len(cuts))
        return jnp.repeat(jnp.exp(heights), shape[axis_at] // blocks).reshape((-1,) + (1,) * (len(shape) - axis_at - 1))

    level = one(*cuts[0])
    for cut in cuts[1:]:
        level = level * one(*cut)
    return level


def length_profile(amount, total, reach, slope):
    loads = [(1 << 20) // math.isqrt(standing ** slope) + 1 for standing in range(2, amount + 1)]
    rest, holding = total - reach - (amount - 1), [1] * (amount - 1)
    while rest > 0:
        candidates = [i for i in range(amount - 1) if holding[i] < reach]
        whole, budget = sum([loads[i] for i in candidates]), rest
        for i in candidates:
            addition = min(reach - holding[i], max(1, budget * loads[i] // whole), rest)
            holding[i] = holding[i] + addition
            rest = rest - addition
    return np.array([reach] + holding)


def uneven(stream_key, count, total, limit, slope):
    if count == 2:
        one = jax.random.randint(stream_key, (), max(1, total - limit), min(limit, total - 1) + 1)
        return jnp.stack([one, total - one])
    lengths = jnp.asarray(length_profile(count, total, limit, slope), jnp.int32)
    twos = (count - 1) // 2
    giver, sink = lengths[1:1 + 2 * twos:2], lengths[2:2 + 2 * twos:2]
    margin = jnp.minimum(giver - 1, limit - sink)
    shifted = jax.random.randint(jax.random.fold_in(stream_key, 1), (twos,), 0, 1 << 20) % (margin + 1)
    lengths = lengths.at[1:1 + 2 * twos:2].set(giver - shifted).at[2:2 + 2 * twos:2].set(sink + shifted)
    return lengths[jax.random.permutation(jax.random.fold_in(stream_key, 2), count)]


def scatter_about(key, dims, width, reach, shards=(), dtype=jnp.bfloat16):
    factor_of = block_levels(key, dims, shards, -0.22, 0.18) if shards else 1.0
    result = jax.random.normal(key, dims, jnp.float32) * width * factor_of
    return jnp.minimum(jnp.maximum(result, -reach), reach).astype(dtype)


def setup_inputs(seed: int = 0) -> dict:
    arg_keys = jax.random.split(jax.random.key(seed), 7)
    return {
        "inputs": scatter_about(arg_keys[0], (TOKENS, D), 1.0, 6.0, ((0, 16),)),
        "segment_ids": jax.vmap(lambda own: jnp.searchsorted(jnp.cumsum(uneven(own, DOCS, SEQ, DOC_MOST, 2)), jnp.arange(SEQ), side="right"))(jax.random.split(arg_keys[1], SEQS)).reshape((SEQS, SEQ)).astype(jnp.int32),
        "cotangent": scatter_about(arg_keys[2], (TOKENS, D), 0.02, 0.125, ((0, 16),)),
        "gains": jnp.clip(1.0 + 0.1 * jax.random.normal(arg_keys[3], (LAYERS, D), jnp.float32), 0.5, 1.5).astype(jnp.bfloat16),
        "w_qkv": scatter_about(arg_keys[4], (LAYERS, D, 3 * ATTN_WIDTH), D ** -0.5, 0.1875, ((0, 16), (1, 16))),
        "w_out": scatter_about(arg_keys[5], (LAYERS, ATTN_WIDTH, D), ATTN_WIDTH ** -0.5, 0.25, ((0, 16), (1, 16))),
    }


def normalize(values, gain):
    centre = lax.optimization_barrier(jnp.mean(values, axis=-1, keepdims=True))
    centred = values - centre
    variance = lax.optimization_barrier(jnp.mean(centred * centred, axis=-1, keepdims=True))
    return centred * lax.rsqrt(variance + 1e-05) * gain

def attend(packed, segment):
    length = packed.shape[0]
    parts = packed.astype(jnp.float32).reshape(length, 3, HEADS, HEAD_DIM)
    queries = parts[:, 0]
    keys_all = parts[:, 1]
    values = parts[:, 2]
    scores = jnp.einsum('qhd,khd->hqk', queries, keys_all) * HEAD_DIM ** (-0.5)
    position = jnp.arange(length)
    allowed = (position[:, None] >= position[None, :]) & (segment[:, None] == segment[None, :])
    scores = jnp.where(allowed[None], scores, -1e+30)
    weights = jnp.exp(scores)
    weights = weights / lax.optimization_barrier(jnp.sum(weights, axis=-1, keepdims=True))
    probs = weights.astype(jnp.bfloat16)
    context = jnp.einsum('hqk,khd->qhd', probs.astype(jnp.float32), values)
    return context.reshape(length, HEADS * HEAD_DIM).astype(jnp.bfloat16)

def forward_layer(hidden, segment, gain, weight_qkv, weight_out):
    normed = normalize(hidden.astype(jnp.float32), gain.astype(jnp.float32)).astype(jnp.bfloat16)
    packed = jnp.dot(normed, weight_qkv, preferred_element_type=jnp.float32).astype(jnp.bfloat16)
    context = attend(packed, segment)
    mixed = jnp.dot(context, weight_out, preferred_element_type=jnp.float32)
    return (hidden.astype(jnp.float32) + mixed).astype(jnp.bfloat16)

def backward_layer(hidden, segment, gain, weight_qkv, weight_out, grad_hidden):
    hidden_f = hidden.astype(jnp.float32)
    gain_f = gain.astype(jnp.float32)
    normed = normalize(hidden_f, gain_f).astype(jnp.bfloat16)
    packed = jnp.dot(normed, weight_qkv, preferred_element_type=jnp.float32).astype(jnp.bfloat16)
    context, attend_back = jax.vjp(lambda inner: attend(inner, segment), packed)
    term_out = lax.dot_general(context, grad_hidden, (((0,), (0,)), ((), ())), preferred_element_type=jnp.float32)
    grad_context = lax.dot_general(grad_hidden, weight_out, (((1,), (1,)), ((), ())), preferred_element_type=jnp.float32).astype(jnp.bfloat16)
    grad_packed = attend_back(grad_context)[0]
    term_qkv = lax.dot_general(normed, grad_packed, (((0,), (0,)), ((), ())), preferred_element_type=jnp.float32)
    grad_normed = lax.dot_general(grad_packed, weight_qkv, (((1,), (1,)), ((), ())), preferred_element_type=jnp.float32)
    _, norm_back = jax.vjp(normalize, hidden_f, gain_f)
    grad_inner, term_gain = norm_back(grad_normed)
    grad_input = (grad_hidden.astype(jnp.float32) + grad_inner).astype(jnp.bfloat16)
    return (grad_input, (term_qkv, term_out, term_gain))

def reference(inputs, segment_ids, cotangent, gains, w_qkv, w_out):
    groups = segment_ids.shape[0] // MICRO
    batches = inputs.reshape(groups, MICRO, SEQ, D)
    segments = segment_ids.reshape(groups, MICRO, SEQ)
    targets = cotangent.reshape(groups, MICRO, SEQ, D)
    empty = (jnp.zeros(w_qkv.shape, jnp.float32), jnp.zeros(w_out.shape, jnp.float32), jnp.zeros(gains.shape, jnp.float32))

    def one_micro(running, items):
        start, segment, target = items

        def forward_pass(hidden, layer_items):
            gain, weight_qkv, weight_out = layer_items
            return (forward_layer(hidden, segment, gain, weight_qkv, weight_out), hidden)
        _, stored = lax.scan(forward_pass, start, (gains, w_qkv, w_out))

        def backward_pass(grad_hidden, layer_items):
            hidden, gain, weight_qkv, weight_out = layer_items
            return backward_layer(hidden, segment, gain, weight_qkv, weight_out, grad_hidden)
        _, layer_terms = lax.scan(backward_pass, target, (stored, gains, w_qkv, w_out), reverse=True)
        return (jax.tree.map(jnp.add, running, layer_terms), None)

    def one_group(totals, items):
        term, _ = lax.scan(one_micro, empty, items)
        rounded = lax.optimization_barrier(jax.tree.map(lambda value: value.astype(jnp.bfloat16), term))
        return (jax.tree.map(lambda total, value: total + value.astype(jnp.float32), totals, rounded), None)
    totals, _ = lax.scan(one_group, empty, (batches, segments, targets))
    return (totals[0], totals[1], totals[2])
```

```python
import functools

import jax
import jax.numpy as jnp
from jax import lax
from jax.experimental import pallas as pl
from jax.experimental.pallas import tpu as pltpu
from jax.sharding import PartitionSpec as P

D = 1024
W = 512
S = 64
STAGE = 4
PAIRS = 4
PACK = 2176
HALF = 1152
SIZES = {"zh": 4, "y": 4, "zl": 2, "x": 4, "core": 2}
BF16 = jnp.bfloat16
F32 = jnp.float32
VMEM_LIMIT = 56 * 1024 * 1024


def dot(a, b, ca, cb):
    return lax.dot_general(a, b, (((ca,), (cb,)), ((), ())), preferred_element_type=F32)


def coords(index):
    out = {}
    for name in ("core", "x", "zl", "y", "zh"):
        out[name] = index % SIZES[name]
        index //= SIZES[name]
    return out


def linear(at):
    index = 0
    for name in ("zh", "y", "zl", "x", "core"):
        index = index * SIZES[name] + at[name]
    return index


def move(value, axis, step, only=None):
    pairs = []
    for index in range(256):
        at = coords(index)
        if only is not None and at["zh"] != only:
            continue
        target = dict(at)
        target[axis] = (at[axis] - step) % SIZES[axis]
        pairs.append((index, linear(target)))
    return lax.ppermute(value, ("section", "dp"), pairs)


def gather_ring(own, axis):
    plus = move(own, axis, 1)
    minus = move(own, axis, -1)
    half = own.shape[0] // 2
    far_a = move(plus[:half], axis, 1)
    far_b = move(minus[half:], axis, -1)
    return own, plus, minus, far_a, far_b


def stack_ring(pieces):
    own, plus, minus, far_a, far_b = pieces
    return jnp.stack([own, plus, jnp.concatenate([far_a, far_b], 0), minus], 0)


def scatter_ring(far, plus, minus, own, axis):
    half = far.shape[0] // 2
    far_a = move(far[:half], axis, -1)
    far_b = move(far[half:], axis, 1)
    plus = jnp.concatenate([add(plus[:half], far_a), plus[half:]], 0)
    minus = jnp.concatenate([minus[:half], add(minus[half:], far_b)], 0)
    from_behind = move(plus, axis, -1)
    from_ahead = move(minus, axis, 1)
    return (own.astype(F32) + from_behind.astype(F32) + from_ahead.astype(F32)).astype(BF16)


def add(a, b):
    return (a.astype(F32) + b.astype(F32)).astype(BF16)


def assemble_kernel(at_ref, *refs):
    pieces = refs[:20]
    wq, wo = refs[20], refs[21]
    sem_q, sem_o = refs[22], refs[23]
    y, zl, x, c = at_ref[0], at_ref[1], at_ref[2], at_ref[3]

    def place(rc, ry, rx, rz):
        layer = lax.rem(y + ry, 4)
        block = lax.rem(zl + rz, 2) * 8 + lax.rem(x + rx, 4) * 2 + lax.rem(c + rc, 2)
        return layer, block

    def put_a(src, *rel):
        layer, block = place(*rel)
        pltpu.make_async_copy(src, wq.at[layer, block, :, pl.ds(0, 1024)], sem_q).start()

    def put_b(src, *rel):
        layer, block = place(*rel)
        pltpu.make_async_copy(
            src.at[:, pl.ds(0, 512)], wq.at[layer, block, :, pl.ds(1024, 512)], sem_q
        ).start()
        pltpu.make_async_copy(
            src.at[pl.ds(0, 32), pl.ds(512, 512)], wo.at[layer, block, :, pl.ds(0, 512)], sem_o
        ).start()
        pltpu.make_async_copy(
            src.at[pl.ds(32, 32), pl.ds(512, 512)], wo.at[layer, block, :, pl.ds(512, 512)], sem_o
        ).start()

    for rc in range(2):
        a = pieces[rc * 10 : rc * 10 + 5]
        b = pieces[rc * 10 + 5 : rc * 10 + 10]
        for rz in range(2):
            for r in range(4):
                put_a(a[0].at[r, rz], rc, 0, r, rz)
                put_a(a[1].at[r, rz], rc, 1, r, rz)
                put_a(a[2].at[r, rz], rc, 3, r, rz)
                put_a(a[3 + r // 2].at[r % 2, rz], rc, 2, r, rz)
                put_b(b[0].at[r, rz], rc, r, 0, rz)
                put_b(b[1].at[r, rz], rc, r, 1, rz)
                put_b(b[2].at[r, rz], rc, r, 3, rz)
                put_b(b[3 + r // 2].at[r % 2, rz], rc, r, 2, rz)
    pltpu.make_async_copy(wq, wq, sem_q).wait()
    pltpu.make_async_copy(wo, wo, sem_o).wait()


def assemble(at, pieces):
    return pl.pallas_call(
        assemble_kernel,
        out_shape=(
            jax.ShapeDtypeStruct((STAGE, 16, 64, 1536), BF16),
            jax.ShapeDtypeStruct((STAGE, 16, 32, 1024), BF16),
        ),
        in_specs=[pl.BlockSpec(memory_space=pltpu.SMEM)] + [pl.BlockSpec(memory_space=pl.ANY)] * 20,
        out_specs=(pl.BlockSpec(memory_space=pltpu.VMEM), pl.BlockSpec(memory_space=pltpu.VMEM)),
        scratch_shapes=[pltpu.SemaphoreType.DMA, pltpu.SemaphoreType.DMA],
        compiler_params=pltpu.CompilerParams(vmem_limit_bytes=VMEM_LIMIT),
        name="assemble",
    )(at, *pieces)


def lane_masks(low, dtype):
    lane = lax.broadcasted_iota(jnp.int32, (S, 128), 1)
    first = jnp.where(lane < 64, low, 0.0).astype(dtype)
    second = jnp.where(lane < 64, 0.0, low).astype(dtype)
    return first, second


def statistics(h):
    centre = jnp.mean(h, axis=-1, keepdims=True)
    centred = h - centre
    variance = jnp.mean(centred * centred, axis=-1, keepdims=True)
    rstd = lax.rsqrt(variance + 1e-05)
    return centred * rstd, rstd


def both_heads(product):
    lane = lax.broadcasted_iota(jnp.int32, (S, 128), 1)
    return jnp.where(lane < 64, product[:S], product[S:])


def forward_kernel(
    active, h_ref, bias_ref, gain_ref, wq, wo, *refs
):
    (h_out, o_h, o_n, o_qkv, o_p, o_c) = refs[5:11]
    (wq_v, wo_v, v_h, v_n, v_qkv, v_p, v_c, sem_w, sem_s) = refs[11:]

    @pl.when(active[0] == 0)
    def _():
        h_out[...] = jnp.zeros_like(h_out)

    @pl.when(active[0] != 0)
    def _():
        for layer in range(STAGE):
            pltpu.make_async_copy(wq.at[layer], wq_v.at[layer], sem_w.at[0, layer]).start()
            pltpu.make_async_copy(wo.at[layer], wo_v.at[layer], sem_w.at[1, layer]).start()
        v_h[0] = h_ref[...]
        bias = bias_ref[...]
        low, high = lane_masks(0.125, BF16)

        def layer_step(layer, carry):
            h = v_h[layer].astype(F32)
            xhat, _ = statistics(h)
            normed = (xhat * gain_ref[layer]).astype(BF16)
            v_n[layer] = normed
            pltpu.make_async_copy(wq.at[layer], wq_v.at[layer], sem_w.at[0, layer]).wait()
            qkv = jnp.dot(normed, wq_v[layer].reshape(D, 3 * W), preferred_element_type=F32).astype(BF16)
            v_qkv[layer] = qkv
            for j in range(PAIRS):
                q = qkv[:, 128 * j : 128 * j + 128]
                k = qkv[:, W + 128 * j : W + 128 * j + 128]
                v = qkv[:, 2 * W + 128 * j : 2 * W + 128 * j + 128]
                q_both = jnp.concatenate([q * low, q * high], 0)
                e = jnp.exp(dot(k, q_both, 1, 1) + bias)
                p = (e * (1.0 / jnp.sum(e, axis=0, keepdims=True))).astype(BF16)
                v_p[layer, :, 128 * j : 128 * j + 128] = p
                v_c[layer, :, 128 * j : 128 * j + 128] = both_heads(dot(p, v, 0, 0)).astype(BF16)
            pltpu.make_async_copy(wo.at[layer], wo_v.at[layer], sem_w.at[1, layer]).wait()
            mixed = jnp.dot(v_c[layer], wo_v[layer].reshape(W, D), preferred_element_type=F32)
            v_h[layer + 1] = (h + mixed).astype(BF16)
            return carry

        lax.fori_loop(0, STAGE, layer_step, 0)
        h_out[...] = v_h[STAGE]
        copies = [
            pltpu.make_async_copy(v_h.at[pl.ds(0, STAGE)], o_h, sem_s.at[0]),
            pltpu.make_async_copy(v_n, o_n, sem_s.at[1]),
            pltpu.make_async_copy(v_qkv, o_qkv, sem_s.at[2]),
            pltpu.make_async_copy(v_p, o_p, sem_s.at[3]),
            pltpu.make_async_copy(v_c, o_c, sem_s.at[4]),
        ]
        for copy in copies:
            copy.start()
        for copy in copies:
            copy.wait()


SAVED = ((STAGE, S, D), (STAGE, S, D), (STAGE, S, 3 * W), (STAGE, S, W), (STAGE, S, W))
KEPT = ((STAGE, S, D), (STAGE, S, 3 * W), (STAGE, S, D))


def forward_stage(active, h, bias, gain, wq, wo, saved):
    smem, vmem, hbm = (
        pl.BlockSpec(memory_space=pltpu.SMEM),
        pl.BlockSpec(memory_space=pltpu.VMEM),
        pl.BlockSpec(memory_space=pl.ANY),
    )
    out = pl.pallas_call(
        forward_kernel,
        out_shape=(jax.ShapeDtypeStruct((S, D), BF16),)
        + tuple(jax.ShapeDtypeStruct(shape, BF16) for shape in SAVED),
        in_specs=[smem, vmem, vmem, vmem, hbm, hbm] + [hbm] * 5,
        out_specs=(vmem,) + (hbm,) * 5,
        input_output_aliases={6 + i: 1 + i for i in range(5)},
        scratch_shapes=[
            pltpu.VMEM((STAGE, 16, 64, 1536), BF16),
            pltpu.VMEM((STAGE, 16, 32, 1024), BF16),
            pltpu.VMEM((STAGE + 1, S, D), BF16),
            pltpu.VMEM(SAVED[1], BF16),
            pltpu.VMEM(SAVED[2], BF16),
            pltpu.VMEM(SAVED[3], BF16),
            pltpu.VMEM(SAVED[4], BF16),
            pltpu.SemaphoreType.DMA((2, STAGE)),
            pltpu.SemaphoreType.DMA((5,)),
        ],
        compiler_params=pltpu.CompilerParams(vmem_limit_bytes=VMEM_LIMIT),
        name="forward_stage",
    )(active, h, bias, gain, wq, wo, *saved)
    return out[0], out[1:]


def backward_kernel(
    active, g_ref, gain_ref, s_h, s_qkv, s_p, wq, wo, *refs
):
    (g_out, o_g, o_d, o_x) = refs[3:7]
    (wq_v, wo_v, v_g, v_d, v_x, sem_w, sem_s) = refs[7:]

    @pl.when(active[0] == 0)
    def _():
        g_out[...] = jnp.zeros_like(g_out)

    @pl.when(active[0] != 0)
    def _():
        for layer in reversed(range(STAGE)):
            pltpu.make_async_copy(wo.at[layer], wo_v.at[layer], sem_w.at[1, layer]).start()
            pltpu.make_async_copy(wq.at[layer], wq_v.at[layer], sem_w.at[0, layer]).start()
        v_g[STAGE] = g_ref[...]
        low, high = lane_masks(1.0, BF16)
        scaled_low, scaled_high = lane_masks(0.125, BF16)

        def layer_step(step, carry):
            layer = STAGE - 1 - step
            g = v_g[layer + 1]
            pltpu.make_async_copy(wo.at[layer], wo_v.at[layer], sem_w.at[1, layer]).wait()
            dctx = dot(g, wo_v[layer].reshape(W, D), 1, 1).astype(BF16)
            for j in range(PAIRS):
                at_q, at_k, at_v = 128 * j, W + 128 * j, 2 * W + 128 * j
                q = s_qkv[layer, :, at_q : at_q + 128]
                k = s_qkv[layer, :, at_k : at_k + 128]
                v = s_qkv[layer, :, at_v : at_v + 128]
                p = s_p[layer, :, 128 * j : 128 * j + 128]
                d = dctx[:, 128 * j : 128 * j + 128]
                d_both = jnp.concatenate([d * low, d * high], 0)
                q_both = jnp.concatenate([q * scaled_low, q * scaled_high], 0)
                dp = dot(v, d_both, 1, 1)
                pf = p.astype(F32)
                t = pf * dp
                ds = (t - pf * jnp.sum(t, axis=0, keepdims=True)).astype(BF16)
                dq = both_heads(dot(ds, k, 0, 0)) * 0.125
                v_d[layer, :, at_q : at_q + 128] = dq.astype(BF16)
                v_d[layer, :, at_k : at_k + 128] = dot(ds, q_both, 1, 0).astype(BF16)
                v_d[layer, :, at_v : at_v + 128] = dot(p, d_both, 1, 0).astype(BF16)
            pltpu.make_async_copy(wq.at[layer], wq_v.at[layer], sem_w.at[0, layer]).wait()
            dn = dot(v_d[layer], wq_v[layer].reshape(D, 3 * W), 1, 1)
            xhat, rstd = statistics(s_h[layer].astype(F32))
            v_x[layer] = (dn * xhat).astype(BF16)
            gd = dn * gain_ref[layer]
            mean_g = jnp.mean(gd, axis=-1, keepdims=True)
            mean_gx = jnp.mean(gd * xhat, axis=-1, keepdims=True)
            v_g[layer] = (g.astype(F32) + rstd * (gd - mean_g - xhat * mean_gx)).astype(BF16)
            return carry

        lax.fori_loop(0, STAGE, layer_step, 0)
        g_out[...] = v_g[0]
        copies = [
            pltpu.make_async_copy(v_g.at[pl.ds(1, STAGE)], o_g, sem_s.at[0]),
            pltpu.make_async_copy(v_d, o_d, sem_s.at[1]),
            pltpu.make_async_copy(v_x, o_x, sem_s.at[2]),
        ]
        for copy in copies:
            copy.start()
        for copy in copies:
            copy.wait()


def backward_stage(active, g, gain, saved, wq, wo, kept):
    smem, vmem, hbm = (
        pl.BlockSpec(memory_space=pltpu.SMEM),
        pl.BlockSpec(memory_space=pltpu.VMEM),
        pl.BlockSpec(memory_space=pl.ANY),
    )
    out = pl.pallas_call(
        backward_kernel,
        out_shape=(jax.ShapeDtypeStruct((S, D), BF16),)
        + tuple(jax.ShapeDtypeStruct(shape, BF16) for shape in KEPT),
        in_specs=[smem, vmem, vmem, vmem, vmem, vmem, hbm, hbm] + [hbm] * 3,
        out_specs=(vmem,) + (hbm,) * 3,
        input_output_aliases={8 + i: 1 + i for i in range(3)},
        scratch_shapes=[
            pltpu.VMEM((STAGE, 16, 64, 1536), BF16),
            pltpu.VMEM((STAGE, 16, 32, 1024), BF16),
            pltpu.VMEM((STAGE + 1, S, D), BF16),
            pltpu.VMEM(KEPT[1], BF16),
            pltpu.VMEM(KEPT[2], BF16),
            pltpu.SemaphoreType.DMA((2, STAGE)),
            pltpu.SemaphoreType.DMA((3,)),
        ],
        compiler_params=pltpu.CompilerParams(vmem_limit_bytes=VMEM_LIMIT),
        name="backward_stage",
    )(active, g, gain, saved[0], saved[2], saved[3], wq, wo, *kept)
    return out[0], out[1:]


def terms_kernel(at_ref, n_ref, c_ref, g_ref, d_ref, x_ref, own_ref, oth_ref):
    zl, x, c = at_ref[1], at_ref[2], at_ref[3]
    first = c == 0

    def place(value, columns, rows):
        lo, count = columns
        at_row, n_rows = rows
        for pair in range(8):
            rz = lax.rem(pair // 4 + zl, 2)
            rx = lax.rem(pair % 4 - x + 4, 4)
            even = value[2 * pair * n_rows : (2 * pair + 1) * n_rows]
            odd = value[(2 * pair + 1) * n_rows : (2 * pair + 2) * n_rows]
            own_ref[rx, rz, at_row : at_row + n_rows, lo : lo + count] = jnp.where(first, even, odd).astype(BF16)
            oth_ref[rx, rz, at_row : at_row + n_rows, lo : lo + count] = jnp.where(first, odd, even).astype(BF16)

    for col in range(0, 1536, 256):
        place(dot(n_ref[0], d_ref[0, :, col : col + 256], 0, 0), (col, 256), (0, 64))
    for half in range(2):
        for col in range(0, 512, 256):
            at = half * 512 + col
            place(dot(c_ref[0], g_ref[0, :, at : at + 256], 0, 0), (1536 + col, 256), (half * 32, 32))
    place(dot(x_ref[0], jnp.ones((S, 128), BF16), 0, 0), (2048, 128), (0, 64))


def terms(at, rel, normed, ctx, g, d, x):
    def pick(width):
        return pl.BlockSpec((1, S, width), lambda i, at: (lax.rem(at[0] + rel, 4), 0, 0))

    shape = (4, 2, 64, PACK)
    return pl.pallas_call(
        terms_kernel,
        out_shape=(jax.ShapeDtypeStruct(shape, BF16),) * 2,
        grid_spec=pltpu.PrefetchScalarGridSpec(
            num_scalar_prefetch=1,
            grid=(1,),
            in_specs=[pick(D), pick(W), pick(D), pick(3 * W), pick(D)],
            out_specs=[pl.BlockSpec(shape, lambda i, at: (0, 0, 0, 0))] * 2,
        ),
        compiler_params=pltpu.CompilerParams(vmem_limit_bytes=VMEM_LIMIT),
        name="weight_terms",
    )(at, normed, ctx, g, d, x)


def body(inputs, segment_ids, cotangent, gains, w_qkv, w_out):
    section = lax.axis_index("section")
    replica = lax.axis_index("dp")
    zh, y = section // 4, section % 4
    zl, x, c = replica // 8, (replica // 2) % 4, replica % 2
    at = jnp.stack([y, zl, x, c]).astype(jnp.int32)

    out_rows = w_out[0]
    packed = jnp.concatenate(
        [w_qkv[0], jnp.concatenate([out_rows[:, :512], out_rows[:, 512:]], 0)], 1
    )
    both = jnp.stack([packed, move(packed, "zl", 1)], 0)
    a_rows = stack_ring(gather_ring(both[:, :, :1024], "x"))
    b_rows = stack_ring(gather_ring(both[:, :, 1024:], "y"))
    a_all = gather_ring(a_rows, "y")
    b_all = gather_ring(b_rows, "x")
    own = tuple(a_all) + tuple(b_all)
    other = tuple(move(piece, "core", 1) for piece in own)
    wq, wo = assemble(at, own + other)
    gain_parts = [gains, move(gains, "y", 1), move(gains, "y", 2), move(gains, "y", 3)]
    gain = jnp.take(jnp.stack(gain_parts, 0), (jnp.arange(4) - y) % 4, axis=0).astype(F32)

    start = lax.dynamic_slice_in_dim(inputs, y * S, S, 0)
    target = lax.dynamic_slice_in_dim(cotangent, y * S, S, 0)
    segment = lax.dynamic_index_in_dim(segment_ids, y, 0, keepdims=False)
    position = jnp.arange(S)
    allowed = (position[:, None] <= position[None, :]) & (segment[:, None] == segment[None, :])
    bias = jnp.where(allowed, 0.0, -1e30).astype(F32)
    bias = jnp.concatenate([bias, bias], 1)

    saved = tuple(jnp.zeros(shape, BF16) for shape in SAVED)
    hidden = start
    for stage in range(4):
        active = (zh == stage).astype(jnp.int32)[None]
        hidden, saved = forward_stage(active, hidden, bias, gain, wq, wo, saved)
        if stage < 3:
            hidden = move(hidden, "zh", -1, only=stage)
    kept = tuple(jnp.zeros(shape, BF16) for shape in KEPT)
    grad = target
    for stage in reversed(range(4)):
        active = (zh == stage).astype(jnp.int32)[None]
        grad, kept = backward_stage(active, grad, gain, saved, wq, wo, kept)
        if stage > 0:
            grad = move(grad, "zh", 1, only=stage)

    sums = {}
    for rel in (2, 1, 3, 0):
        own_term, other_term = terms(at, rel, saved[1], saved[4], kept[0], kept[1], kept[2])
        sums[rel] = add(own_term, move(other_term, "core", 1))
    a = {rel: sums[rel][..., :HALF] for rel in sums}
    a_y = scatter_ring(a[2], a[1], a[3], a[0], "y")
    a_x = scatter_ring(a_y[2], a_y[1], a_y[3], a_y[0], "x")
    b = {rx: jnp.stack([sums[ry][rx, :, :, HALF:] for ry in range(4)], 0) for rx in range(4)}
    b_x = scatter_ring(b[2], b[1], b[3], b[0], "x")
    b_y = scatter_ring(b_x[2], b_x[1], b_x[3], b_x[0], "y")
    last = jnp.concatenate([a_x, b_y], -1)
    total = last[0].astype(F32) + move(last[1], "zl", 1).astype(F32)
    grad_out = jnp.concatenate([total[:32, 1536:2048], total[32:, 1536:2048]], 1)
    return total[None, :, :1536], grad_out[None], total[:, 2048][None]


def solution(mesh):
    placed = (
        P("dp", None),
        P("dp", None),
        P("dp", None),
        P("section", None),
        P("section", "dp", None),
        P("section", "dp", None),
    )
    return jax.shard_map(
        body,
        mesh=mesh,
        in_specs=placed,
        out_specs=(P("section", "dp", None), P("section", "dp", None), P("section", "dp")),
        check_vma=False,
    )
```

```python
import functools

import jax
import jax.numpy as jnp
from jax import lax
from jax.experimental import pallas as pl
from jax.experimental.pallas import tpu as pltpu
from jax.sharding import PartitionSpec as P

D = 1024
W = 512
S = 64
STAGE = 4
PAIRS = 4
PACK = 2176
HALF = 1152
SIZES = {"zh": 4, "y": 4, "zl": 2, "x": 4, "core": 2}
BF16 = jnp.bfloat16
F32 = jnp.float32
STAGE_LIMIT = 8 * 1024 * 1024
TERMS_LIMIT = 24 * 1024 * 1024


def dot(a, b, ca, cb):
    return lax.dot_general(a, b, (((ca,), (cb,)), ((), ())), preferred_element_type=F32)


def coords(index):
    out = {}
    for name in ("core", "x", "zl", "y", "zh"):
        out[name] = index % SIZES[name]
        index //= SIZES[name]
    return out


def linear(at):
    index = 0
    for name in ("zh", "y", "zl", "x", "core"):
        index = index * SIZES[name] + at[name]
    return index


def move(value, axis, step, only=None):
    pairs = []
    for index in range(256):
        at = coords(index)
        if only is not None and at["zh"] != only:
            continue
        target = dict(at)
        far = step[at["core"]] if isinstance(step, tuple) else step
        target[axis] = (at[axis] - far) % SIZES[axis]
        pairs.append((index, linear(target)))
    return lax.ppermute(value, ("section", "dp"), pairs)


def gather_rings(first, *rings):
    near = [(move(own, axis, 1), move(own, axis, -1)) for own, axis in rings]
    near = lax.optimization_barrier(near)
    out = []
    for (own, axis), (plus, minus) in zip(rings, near, strict=True):
        far = move(jnp.where(first, plus, minus), axis, (1, -1))
        out.append([own, plus, far, minus])
    return out


def scatter_rings(first, *rings):
    passing = [move(far, axis, (-1, 1)) for far, _, _, _, axis in rings]
    out = []
    for (_, plus, minus, own, axis), far in zip(rings, passing, strict=True):
        zero = jnp.zeros_like(far)
        behind = move(add(plus, jnp.where(first, far, zero)), axis, -1)
        ahead = move(add(minus, jnp.where(first, zero, far)), axis, 1)
        out.append(add(own, behind, ahead))
    return out


def add(*values):
    return functools.reduce(jnp.add, [value.astype(F32) for value in values]).astype(BF16)


WEIGHT = (STAGE, 2, 4, 2, 64, 1024)
SAVED = ((STAGE, S, D), (STAGE, S, D), (STAGE, S, 3 * W), (STAGE, S, W), (STAGE, S, W))
KEPT = ((STAGE, S, D), (STAGE, S, 3 * W), (STAGE, S, D))
SMEM_SPEC = pl.BlockSpec(memory_space=pltpu.SMEM)
VMEM_SPEC = pl.BlockSpec(memory_space=pltpu.VMEM)
ANY_SPEC = pl.BlockSpec(memory_space=pl.ANY)


def in_vmem(*arrays):
    return tuple(pltpu.with_memory_space_constraint(array, pltpu.VMEM) for array in arrays)


def lane_masks(low, dtype):
    lane = lax.broadcasted_iota(jnp.int32, (S, 128), 1)
    first = jnp.where(lane < 64, low, 0.0).astype(dtype)
    second = jnp.where(lane < 64, 0.0, low).astype(dtype)
    return first, second


def statistics(h):
    centre = jnp.mean(h, axis=-1, keepdims=True)
    centred = h - centre
    variance = jnp.mean(centred * centred, axis=-1, keepdims=True)
    rstd = lax.rsqrt(variance + 1e-05)
    return centred * rstd, rstd


def both_heads(product):
    lane = lax.broadcasted_iota(jnp.int32, (S, 128), 1)
    return jnp.where(lane < 64, product[:S], product[S:])


def weights_of(wa, wb, layer):
    both = wb[layer].reshape(16, 64, 1024)
    return (
        wa[layer].reshape(D, 2 * W),
        both[:, :, :W].reshape(D, W),
        both[:, :32, W:].reshape(W, W),
        both[:, 32:, W:].reshape(W, W),
    )


def piece_at(pieces, outer, inner):
    return pieces[outer].at[inner]


def load_weights(at, pieces, wa, wb, sem):
    y, x, c = at[0], at[2], at[3]

    def one_layer(layer, carry):
        rel = lax.rem(layer - y + 4, 4)
        for ry in range(4):

            @pl.when(rel == ry)
            def _():
                for rc in range(2):
                    core = lax.rem(c + rc, 2)
                    for rx in range(4):
                        column = lax.rem(x + rx, 4)
                        a = piece_at(pieces[rc * 8 : rc * 8 + 4], ry, rx)
                        pltpu.make_async_copy(a, wa.at[layer, :, column, core], sem.at[0, layer]).start()
                        b = piece_at(pieces[rc * 8 + 4 : rc * 8 + 8], rx, ry)
                        pltpu.make_async_copy(b, wb.at[layer, :, column, core], sem.at[1, layer]).start()

        return carry

    lax.fori_loop(0, STAGE, one_layer, 0)


def wait_weights(which, layer, ref, sem):
    pltpu.make_async_copy(ref.at[layer], ref.at[layer], sem.at[which, layer]).wait()


def forward_kernel(stage, at, h_ref, bias_ref, gain_ref, *refs):
    first = stage == 0
    if first:
        pieces, refs = refs[:16], refs[16:]
        wa, wb, h_out, o_h, o_n, o_qkv, o_p, o_c, sem = refs
        load_weights(at, pieces, wa, wb, sem)
    else:
        wa, wb, h_out, o_h, o_n, o_qkv, o_p, o_c = refs[7:]

    @pl.when(at[4] != stage)
    def _():
        h_out[...] = jnp.zeros_like(h_out)
        if first:
            for layer in range(STAGE):
                wait_weights(0, layer, wa, sem)
                wait_weights(1, layer, wb, sem)

    @pl.when(at[4] == stage)
    def _():
        h_out[...] = h_ref[...]
        bias = bias_ref[...]
        low, high = lane_masks(0.125, BF16)

        def layer_step(layer, carry):
            hidden = h_out[...]
            o_h[layer] = hidden
            h = hidden.astype(F32)
            xhat, _ = statistics(h)
            normed = (xhat * gain_ref[layer]).astype(BF16)
            o_n[layer] = normed
            if first:
                wait_weights(0, layer, wa, sem)
            qk = jnp.dot(normed, wa[layer].reshape(D, 2 * W), preferred_element_type=F32).astype(BF16)
            o_qkv[layer, :, : 2 * W] = qk
            if first:
                wait_weights(1, layer, wb, sem)
            _, w_value, out_left, out_right = weights_of(wa, wb, layer)
            value = jnp.dot(normed, w_value, preferred_element_type=F32).astype(BF16)
            o_qkv[layer, :, 2 * W :] = value
            parts = []
            for j in range(PAIRS):
                q = qk[:, 128 * j : 128 * j + 128]
                k = qk[:, W + 128 * j : W + 128 * j + 128]
                q_both = jnp.concatenate([q * low, q * high], 0)
                e = jnp.exp(dot(k, q_both, 1, 1) + bias)
                p = (e * (1.0 / jnp.sum(e, axis=0, keepdims=True))).astype(BF16)
                o_p[layer, :, 128 * j : 128 * j + 128] = p
                parts.append(both_heads(dot(p, value[:, 128 * j : 128 * j + 128], 0, 0)).astype(BF16))
            ctx = jnp.concatenate(parts, 1)
            o_c[layer] = ctx
            left = jnp.dot(ctx, out_left, preferred_element_type=F32)
            right = jnp.dot(ctx, out_right, preferred_element_type=F32)
            h_out[:, :W] = (h[:, :W] + left).astype(BF16)
            h_out[:, W:] = (h[:, W:] + right).astype(BF16)
            return carry

        lax.fori_loop(0, STAGE, layer_step, 0)


def forward_stage(stage, at, h, bias, gain, weights, saved, pieces):
    first = stage == 0
    out = [pltpu.VMEM(WEIGHT, BF16)] * 2 + [pltpu.VMEM((S, D), BF16)]
    out += [pltpu.VMEM(shape, BF16) for shape in SAVED]
    args = [at, *in_vmem(h, bias, gain)]
    specs = [SMEM_SPEC, VMEM_SPEC, VMEM_SPEC, VMEM_SPEC]
    if first:
        args += [pltpu.with_memory_space_constraint(piece, pltpu.HBM) for piece in pieces]
        specs += [ANY_SPEC] * 16
        aliases, scratch = {}, [pltpu.SemaphoreType.DMA((2, STAGE))]
    else:
        args += list(in_vmem(*weights, *saved))
        specs += [VMEM_SPEC] * 7
        aliases, scratch = {4: 0, 5: 1} | {6 + i: 3 + i for i in range(5)}, []
    result = pl.pallas_call(
        functools.partial(forward_kernel, stage),
        out_shape=tuple(out),
        in_specs=specs,
        out_specs=(VMEM_SPEC,) * len(out),
        input_output_aliases=aliases,
        scratch_shapes=scratch,
        compiler_params=pltpu.CompilerParams(vmem_limit_bytes=STAGE_LIMIT),
        name="forward_stage",
    )(*args)
    return result[:2], result[2], result[3:]


def backward_kernel(stage, at, g_ref, gain_ref, s_h, s_qkv, s_p, *refs):
    wa, wb, g_out, o_g, o_d, o_x = refs[2:] if stage == 3 else refs[5:]

    @pl.when(at[4] != stage)
    def _():
        g_out[...] = jnp.zeros_like(g_out)

    @pl.when(at[4] == stage)
    def _():
        g_out[...] = g_ref[...]
        low, high = lane_masks(1.0, BF16)
        scaled_low, scaled_high = lane_masks(0.125, BF16)

        def layer_step(step, carry):
            layer = STAGE - 1 - step
            g = g_out[...]
            o_g[layer] = g
            w_qk, w_value, out_left, out_right = weights_of(wa, wb, layer)
            dctx = (dot(g[:, :W], out_left, 1, 1) + dot(g[:, W:], out_right, 1, 1)).astype(BF16)
            for j in range(PAIRS):
                at_q, at_k, at_v = 128 * j, W + 128 * j, 2 * W + 128 * j
                q = s_qkv[layer, :, at_q : at_q + 128]
                k = s_qkv[layer, :, at_k : at_k + 128]
                v = s_qkv[layer, :, at_v : at_v + 128]
                p = s_p[layer, :, 128 * j : 128 * j + 128]
                d = dctx[:, 128 * j : 128 * j + 128]
                d_both = jnp.concatenate([d * low, d * high], 0)
                q_both = jnp.concatenate([q * scaled_low, q * scaled_high], 0)
                dp = dot(v, d_both, 1, 1)
                pf = p.astype(F32)
                t = pf * dp
                ds = (t - pf * jnp.sum(t, axis=0, keepdims=True)).astype(BF16)
                dq = both_heads(dot(ds, k, 0, 0)) * 0.125
                o_d[layer, :, at_q : at_q + 128] = dq.astype(BF16)
                o_d[layer, :, at_k : at_k + 128] = dot(ds, q_both, 1, 0).astype(BF16)
                o_d[layer, :, at_v : at_v + 128] = dot(p, d_both, 1, 0).astype(BF16)
            dn = dot(o_d[layer, :, : 2 * W], w_qk, 1, 1) + dot(o_d[layer, :, 2 * W :], w_value, 1, 1)
            xhat, rstd = statistics(s_h[layer].astype(F32))
            o_x[layer] = (dn * xhat).astype(BF16)
            gd = dn * gain_ref[layer]
            mean_g = jnp.mean(gd, axis=-1, keepdims=True)
            mean_gx = jnp.mean(gd * xhat, axis=-1, keepdims=True)
            g_out[...] = (g.astype(F32) + rstd * (gd - mean_g - xhat * mean_gx)).astype(BF16)
            return carry

        lax.fori_loop(0, STAGE, layer_step, 0)


def backward_stage(stage, at, g, gain, saved, weights, kept):
    first = stage == 3
    args = in_vmem(g, gain, saved[0], saved[2], saved[3], *weights, *(() if first else kept))
    out = (pltpu.VMEM(WEIGHT, BF16),) * 2 + (pltpu.VMEM((S, D), BF16),)
    out += tuple(pltpu.VMEM(shape, BF16) for shape in KEPT)
    result = pl.pallas_call(
        functools.partial(backward_kernel, stage),
        out_shape=out,
        in_specs=[SMEM_SPEC] + [VMEM_SPEC] * len(args),
        out_specs=(VMEM_SPEC,) * len(out),
        input_output_aliases={6: 0, 7: 1} | ({} if first else {8 + i: 3 + i for i in range(3)}),
        compiler_params=pltpu.CompilerParams(vmem_limit_bytes=STAGE_LIMIT),
        name="backward_stage",
    )(at, *args)
    return result[:2], result[2], result[3:]


def swap_blocks(value, size, swap):
    lane = lax.broadcasted_iota(jnp.int32, value.shape, 1)
    width = value.shape[1]
    swapped = jnp.where(
        lax.rem(lane, 2 * size) < size,
        pltpu.roll(value, width - size, 1),
        pltpu.roll(value, size, 1),
    )
    return jnp.where(swap, swapped, value)


def terms_kernel(at_ref, n_ref, c_ref, g_ref, d_ref, x_ref, own_ref, oth_ref):
    zl, x, c = at_ref[1], at_ref[2], at_ref[3]
    swap = c == 1
    normed = swap_blocks(n_ref[0].astype(F32), 64, swap).astype(BF16)
    ctx = swap_blocks(c_ref[0].astype(F32), 32, swap).astype(BF16)
    scaled = swap_blocks(x_ref[0].astype(F32), 64, swap).astype(BF16)

    def place(value, lo, at_row, rows):
        value = value.astype(BF16)
        count = value.shape[1]
        for pair in range(8):
            rz = lax.rem(pair // 4 + zl, 2)
            rx = lax.rem(pair % 4 - x + 4, 4)
            for which, ref in enumerate((own_ref, oth_ref)):
                at = (2 * pair + which) * rows
                ref[rx, rz, at_row : at_row + rows, lo : lo + count] = value[at : at + rows]

    for col in range(0, 1536, 256):
        place(dot(normed, d_ref[0, :, col : col + 256], 0, 0), col, 0, 64)
    for half in range(2):
        for col in range(0, 512, 256):
            at = half * 512 + col
            place(dot(ctx, g_ref[0, :, at : at + 256], 0, 0), 1536 + col, half * 32, 32)
    place(dot(scaled, jnp.ones((S, 128), BF16), 0, 0), 2048, 0, 64)


def terms(at, rel, normed, ctx, g, d, x):
    def pick(width):
        return pl.BlockSpec((1, S, width), lambda i, at: (lax.rem(at[0] + rel, 4), 0, 0))

    shape = (4, 2, 64, PACK)
    return pl.pallas_call(
        terms_kernel,
        out_shape=(jax.ShapeDtypeStruct(shape, BF16),) * 2,
        grid_spec=pltpu.PrefetchScalarGridSpec(
            num_scalar_prefetch=1,
            grid=(1,),
            in_specs=[pick(D), pick(W), pick(D), pick(3 * W), pick(D)],
            out_specs=[pl.BlockSpec(shape, lambda i, at: (0, 0, 0, 0))] * 2,
        ),
        compiler_params=pltpu.CompilerParams(vmem_limit_bytes=TERMS_LIMIT),
        name="weight_terms",
    )(at, normed, ctx, g, d, x)


def body(inputs, segment_ids, cotangent, gains, w_qkv, w_out):
    section = lax.axis_index("section")
    replica = lax.axis_index("dp")
    zh, y = section // 4, section % 4
    zl, x, c = replica // 8, (replica // 2) % 4, replica % 2
    at = jnp.stack([y, zl, x, c, zh]).astype(jnp.int32)

    out_rows = w_out[0]
    packed = jnp.concatenate(
        [w_qkv[0], jnp.concatenate([out_rows[:, :512], out_rows[:, 512:]], 0)], 1
    )
    opposite = move(packed, "zl", 1)
    upper = zl == 1
    both = jnp.stack([jnp.where(upper, opposite, packed), jnp.where(upper, packed, opposite)], 0)
    gain_rows = jnp.broadcast_to(jnp.pad(gains, ((0, 15), (0, 0)))[None], (2, 16, D))
    first = c == 0
    a_near, b_near = gather_rings(
        first, (both[:, :, :1024], "x"), (jnp.concatenate([both[:, :, 1024:], gain_rows], 1), "y")
    )
    gain_parts = jnp.stack([block[0, 64] for block in b_near], 0)
    gain = jnp.take(gain_parts, (jnp.arange(4) - y) % 4, axis=0).astype(F32)[:, None]

    start = lax.dynamic_slice_in_dim(inputs, y * S, S, 0)
    target = lax.dynamic_slice_in_dim(cotangent, y * S, S, 0)
    segment = lax.dynamic_index_in_dim(segment_ids, y, 0, keepdims=False)
    position = jnp.arange(S)
    allowed = (position[:, None] <= position[None, :]) & (segment[:, None] == segment[None, :])
    bias = jnp.where(allowed, 0.0, -1e30).astype(F32)
    bias = jnp.concatenate([bias, bias], 1)

    rows = jnp.stack(a_near, 0), jnp.stack([block[:, :64] for block in b_near], 0)
    rows, at, gain, bias, start, target = lax.optimization_barrier((rows, at, gain, bias, start, target))
    a_all, b_all = gather_rings(first, (rows[0], "y"), (rows[1], "x"))
    own = a_all + b_all
    pieces = own + [move(piece, "core", 1) for piece in own]

    weights = saved = kept = None
    hidden, grad = start, target
    for stage in range(4):
        weights, hidden, saved = forward_stage(stage, at, hidden, bias, gain, weights, saved, pieces)
        if stage < 3:
            hidden = move(hidden, "zh", -1, only=stage)
    for stage in reversed(range(4)):
        weights, grad, kept = backward_stage(stage, at, grad, gain, saved, weights, kept)
        if stage > 0:
            grad = move(grad, "zh", 1, only=stage)

    sums = {}
    for rel in (2, 1, 3, 0):
        own_term, other_term = terms(at, rel, saved[1], saved[4], kept[0], kept[1], kept[2])
        sums[rel] = add(own_term, move(other_term, "core", 1))
    a = {rel: sums[rel][..., :HALF] for rel in sums}
    b = {rx: jnp.stack([sums[ry][rx, :, :, HALF:] for ry in range(4)], 0) for rx in range(4)}
    a_y, b_x = scatter_rings(first, (a[2], a[1], a[3], a[0], "y"), (b[2], b[1], b[3], b[0], "x"))
    a_x, b_y = scatter_rings(
        first, (a_y[2], a_y[1], a_y[3], a_y[0], "x"), (b_x[2], b_x[1], b_x[3], b_x[0], "y")
    )
    last = jnp.concatenate([a_x, b_y], -1)
    total = last[0].astype(F32) + move(last[1], "zl", 1).astype(F32)
    grad_out = jnp.concatenate([total[:32, 1536:2048], total[32:, 1536:2048]], 1)
    return total[None, :, :1536], grad_out[None], total[:, 2048][None]


def solution(mesh):
    placed = (
        P("dp", None),
        P("dp", None),
        P("dp", None),
        P("section", None),
        P("section", "dp", None),
        P("section", "dp", None),
    )
    return jax.shard_map(
        body,
        mesh=mesh,
        in_specs=placed,
        out_specs=(P("section", "dp", None), P("section", "dp", None), P("section", "dp")),
        check_vma=False,
    )
```

```python
import functools

import jax
import jax.numpy as jnp
from jax import lax
from jax.experimental import pallas as pl
from jax.experimental.pallas import tpu as pltpu
from jax.sharding import PartitionSpec as P

D = 1024
W = 512
S = 64
STAGE = 4
FOUR = 256
PACK = 2176
HALF = 1152
SIZES = {"zh": 4, "y": 4, "zl": 2, "x": 4, "core": 2}
BF16 = jnp.bfloat16
F32 = jnp.float32
STAGE_LIMIT = 8 * 1024 * 1024
TERMS_LIMIT = 24 * 1024 * 1024


def dot(a, b, ca, cb):
    return lax.dot_general(a, b, (((ca,), (cb,)), ((), ())), preferred_element_type=F32)


def coords(index):
    out = {}
    for name in ("core", "x", "zl", "y", "zh"):
        out[name] = index % SIZES[name]
        index //= SIZES[name]
    return out


def linear(at):
    index = 0
    for name in ("zh", "y", "zl", "x", "core"):
        index = index * SIZES[name] + at[name]
    return index


def move(value, axis, step, only=None):
    pairs = []
    for index in range(256):
        at = coords(index)
        if only is not None and at["zh"] != only:
            continue
        target = dict(at)
        far = step[at["core"]] if isinstance(step, tuple) else step
        target[axis] = (at[axis] - far) % SIZES[axis]
        pairs.append((index, linear(target)))
    return lax.ppermute(value, ("section", "dp"), pairs)


def gather_rings(first, *rings):
    near = [(move(own, axis, 1), move(own, axis, -1)) for own, axis in rings]
    near = lax.optimization_barrier(near)
    out = []
    for (own, axis), (plus, minus) in zip(rings, near, strict=True):
        far = move(jnp.where(first, plus, minus), axis, (1, -1))
        out.append([own, plus, far, minus])
    return out


def scatter_rings(first, *rings):
    passing = [move(far, axis, (-1, 1)) for far, _, _, _, axis in rings]
    out = []
    for (_, plus, minus, own, axis), far in zip(rings, passing, strict=True):
        zero = jnp.zeros_like(far)
        behind = move(add(plus, jnp.where(first, far, zero)), axis, -1)
        ahead = move(add(minus, jnp.where(first, zero, far)), axis, 1)
        out.append(add(own, behind, ahead))
    return out


def add(*values):
    return functools.reduce(jnp.add, [value.astype(F32) for value in values]).astype(BF16)


WEIGHT = (STAGE, 2, 4, 2, 64, 1024)
SAVED = ((STAGE, S, D), (STAGE, S, D), (STAGE, S, 3 * W), (STAGE, S, W), (STAGE, S, W))
KEPT = ((STAGE, S, D), (STAGE, S, 3 * W), (STAGE, S, D))
SMEM_SPEC = pl.BlockSpec(memory_space=pltpu.SMEM)
VMEM_SPEC = pl.BlockSpec(memory_space=pltpu.VMEM)
ANY_SPEC = pl.BlockSpec(memory_space=pl.ANY)


def in_vmem(*arrays):
    return tuple(pltpu.with_memory_space_constraint(array, pltpu.VMEM) for array in arrays)


def head_masks(value):
    head = lax.broadcasted_iota(jnp.int32, (S, FOUR), 1) // 64
    return [jnp.where(head == i, value, 0.0).astype(BF16) for i in range(4)]


def spread(value, masks):
    return jnp.concatenate([value * mask for mask in masks], 0)


def collect(product):
    head = lax.broadcasted_iota(jnp.int32, (S, FOUR), 1) // 64
    out = product[3 * S :]
    for i in (2, 1, 0):
        out = jnp.where(head == i, product[i * S : (i + 1) * S], out)
    return out


def statistics(h):
    centre = jnp.mean(h, axis=-1, keepdims=True)
    centred = h - centre
    variance = jnp.mean(centred * centred, axis=-1, keepdims=True)
    rstd = lax.rsqrt(variance + 1e-05)
    return centred * rstd, rstd


def weights_of(wa, wb, layer):
    both = wb[layer].reshape(16, 64, 1024)
    return (
        wa[layer].reshape(D, 2 * W),
        both[:, :, :W].reshape(D, W),
        both[:, :32, W:].reshape(W, W),
        both[:, 32:, W:].reshape(W, W),
    )


def piece_at(pieces, outer, inner):
    return pieces[outer].at[inner]


def load_weights(at, pieces, wa, wb, sem, far):
    y, x, c = at[0], at[2], at[3]

    def one_layer(layer, carry):
        rel = lax.rem(layer - y + 4, 4)
        for ry in range(4):

            @pl.when(rel == ry)
            def _():
                for rc in range(2):
                    core = lax.rem(c + rc, 2)
                    for rx in range(4):
                        column = lax.rem(x + rx, 4)
                        if (ry == 2) == far:
                            a = piece_at(pieces[rc * 8 : rc * 8 + 4], ry, rx)
                            pltpu.make_async_copy(a, wa.at[layer, :, column, core], sem.at[0, layer]).start()
                        if (rx == 2) == far:
                            b = piece_at(pieces[rc * 8 + 4 : rc * 8 + 8], rx, ry)
                            pltpu.make_async_copy(b, wb.at[layer, :, column, core], sem.at[1, layer]).start()

        return carry

    lax.fori_loop(0, STAGE, one_layer, 0)


def wait_weights(at, layer, wa, wb, sem, far):
    @pl.when((lax.rem(layer - at[0] + 4, 4) == 2) == far)
    def _():
        pltpu.make_async_copy(wa.at[layer], wa.at[layer], sem.at[0, layer]).wait()

    some = wb.at[layer, :, pl.ds(0, 1 if far else 3)]
    pltpu.make_async_copy(some, some, sem.at[1, layer]).wait()


def load_kernel(at, *refs):
    pieces, (wa, wb, sem) = refs[:16], refs[16:]
    load_weights(at, pieces, wa, wb, sem, False)
    for layer in range(STAGE):
        wait_weights(at, layer, wa, wb, sem, False)


def load_near(at, pieces):
    near = [pieces[i] if i % 4 != 2 else pieces[i - 1] for i in range(16)]
    near = [pltpu.with_memory_space_constraint(piece, pltpu.HBM) for piece in near]
    return pl.pallas_call(
        load_kernel,
        out_shape=(pltpu.VMEM(WEIGHT, BF16),) * 2,
        in_specs=[SMEM_SPEC] + [ANY_SPEC] * 16,
        out_specs=(VMEM_SPEC,) * 2,
        scratch_shapes=[pltpu.SemaphoreType.DMA((2, STAGE))],
        compiler_params=pltpu.CompilerParams(vmem_limit_bytes=STAGE_LIMIT),
        cost_estimate=pl.CostEstimate(flops=0, bytes_accessed=24 * D * D, transcendentals=0),
        name="load_near",
    )(at, *near)


def forward_kernel(stage, at, h_ref, bias_ref, gain_ref, *refs):
    first = stage == 0
    if first:
        pieces = [refs[2 + i // 4] if i % 4 == 2 else None for i in range(16)]
        wa, wb, h_out, o_h, o_n, o_qkv, o_p, o_c, sem = refs[6:]
        load_weights(at, pieces, wa, wb, sem, True)
    else:
        wa, wb, h_out, o_h, o_n, o_qkv, o_p, o_c = refs[7:]

    @pl.when(at[4] != stage)
    def _():
        h_out[...] = jnp.zeros_like(h_out)
        if first:
            for layer in range(STAGE):
                wait_weights(at, layer, wa, wb, sem, True)

    @pl.when(at[4] == stage)
    def _():
        h_out[...] = h_ref[...]
        bias = bias_ref[...]
        masks = head_masks(0.125)

        def layer_step(layer, carry):
            hidden = h_out[...]
            o_h[layer] = hidden
            h = hidden.astype(F32)
            xhat, _ = statistics(h)
            normed = (xhat * gain_ref[layer]).astype(BF16)
            o_n[layer] = normed
            if first:
                wait_weights(at, layer, wa, wb, sem, True)
            qk = jnp.dot(normed, wa[layer].reshape(D, 2 * W), preferred_element_type=F32).astype(BF16)
            o_qkv[layer, :, : 2 * W] = qk
            _, w_value, out_left, out_right = weights_of(wa, wb, layer)
            value = jnp.dot(normed, w_value, preferred_element_type=F32).astype(BF16)
            o_qkv[layer, :, 2 * W :] = value
            parts = []
            for at_head in range(0, W, FOUR):
                cut = slice(at_head, at_head + FOUR)
                e = jnp.exp(dot(qk[:, W:][:, cut], spread(qk[:, cut], masks), 1, 1) + bias)
                p = (e * (1.0 / jnp.sum(e, axis=0, keepdims=True))).astype(BF16)
                o_p[layer, :, cut] = p
                parts.append(collect(dot(p, value[:, cut], 0, 0)).astype(BF16))
            ctx = jnp.concatenate(parts, 1)
            o_c[layer] = ctx
            left = jnp.dot(ctx, out_left, preferred_element_type=F32)
            right = jnp.dot(ctx, out_right, preferred_element_type=F32)
            h_out[:, :W] = (h[:, :W] + left).astype(BF16)
            h_out[:, W:] = (h[:, W:] + right).astype(BF16)
            return carry

        lax.fori_loop(0, STAGE, layer_step, 0)


def forward_stage(stage, at, h, bias, gain, weights, saved, pieces):
    first = stage == 0
    out = [pltpu.VMEM(WEIGHT, BF16)] * 2 + [pltpu.VMEM((S, D), BF16)]
    out += [pltpu.VMEM(shape, BF16) for shape in SAVED]
    args = [at, *in_vmem(h, bias, gain)]
    specs = [SMEM_SPEC, VMEM_SPEC, VMEM_SPEC, VMEM_SPEC]
    args += list(in_vmem(*weights))
    specs += [VMEM_SPEC] * 2
    if first:
        args += [pieces[i] for i in range(16) if i % 4 == 2]
        specs += [ANY_SPEC] * 4
        aliases, scratch = {4: 0, 5: 1}, [pltpu.SemaphoreType.DMA((2, STAGE))]
    else:
        args += list(in_vmem(*saved))
        specs += [VMEM_SPEC] * 5
        aliases, scratch = {4: 0, 5: 1} | {6 + i: 3 + i for i in range(5)}, []
    result = pl.pallas_call(
        functools.partial(forward_kernel, stage),
        out_shape=tuple(out),
        in_specs=specs,
        out_specs=(VMEM_SPEC,) * len(out),
        input_output_aliases=aliases,
        scratch_shapes=scratch,
        compiler_params=pltpu.CompilerParams(vmem_limit_bytes=STAGE_LIMIT),
        name="forward_stage",
    )(*args)
    return result[:2], result[2], result[3:]


def backward_kernel(stage, at, g_ref, gain_ref, s_h, s_qkv, s_p, *refs):
    wa, wb, g_out, o_g, o_d, o_x = refs[2:] if stage == 3 else refs[5:]

    @pl.when(at[4] != stage)
    def _():
        g_out[...] = jnp.zeros_like(g_out)

    @pl.when(at[4] == stage)
    def _():
        g_out[...] = g_ref[...]
        masks, scaled = head_masks(1.0), head_masks(0.125)

        def layer_step(step, carry):
            layer = STAGE - 1 - step
            g = g_out[...]
            o_g[layer] = g
            w_qk, w_value, out_left, out_right = weights_of(wa, wb, layer)
            dctx = (dot(g[:, :W], out_left, 1, 1) + dot(g[:, W:], out_right, 1, 1)).astype(BF16)
            both = []
            for lo in range(0, W, FOUR):
                d_rows = spread(dctx[:, lo : lo + FOUR], masks)
                p = s_p[layer, :, lo : lo + FOUR]
                pf = p.astype(F32)
                t = pf * dot(s_qkv[layer, :, 2 * W + lo : 2 * W + lo + FOUR], d_rows, 1, 1)
                o_d[layer, :, 2 * W + lo : 2 * W + lo + FOUR] = dot(p, d_rows, 1, 0).astype(BF16)
                both.append((t - pf * jnp.sum(t, axis=0, keepdims=True)).astype(BF16))
            for lo, ds in zip(range(0, W, FOUR), both, strict=True):
                q_rows = spread(s_qkv[layer, :, lo : lo + FOUR], scaled)
                o_d[layer, :, W + lo : W + lo + FOUR] = dot(ds, q_rows, 1, 0).astype(BF16)
            for lo, ds in zip(range(0, W, FOUR), both, strict=True):
                dq = collect(dot(ds, s_qkv[layer, :, W + lo : W + lo + FOUR], 0, 0)) * 0.125
                o_d[layer, :, lo : lo + FOUR] = dq.astype(BF16)
            dn = dot(o_d[layer, :, 2 * W :], w_value, 1, 1) + dot(o_d[layer, :, : 2 * W], w_qk, 1, 1)
            xhat, rstd = statistics(s_h[layer].astype(F32))
            o_x[layer] = (dn * xhat).astype(BF16)
            gd = dn * gain_ref[layer]
            mean_g = jnp.mean(gd, axis=-1, keepdims=True)
            mean_gx = jnp.mean(gd * xhat, axis=-1, keepdims=True)
            g_out[...] = (g.astype(F32) + rstd * (gd - mean_g - xhat * mean_gx)).astype(BF16)
            return carry

        lax.fori_loop(0, STAGE, layer_step, 0)


def backward_stage(stage, at, g, gain, saved, weights, kept):
    first = stage == 3
    args = in_vmem(g, gain, saved[0], saved[2], saved[3], *weights, *(() if first else kept))
    out = (pltpu.VMEM(WEIGHT, BF16),) * 2 + (pltpu.VMEM((S, D), BF16),)
    out += tuple(pltpu.VMEM(shape, BF16) for shape in KEPT)
    result = pl.pallas_call(
        functools.partial(backward_kernel, stage),
        out_shape=out,
        in_specs=[SMEM_SPEC] + [VMEM_SPEC] * len(args),
        out_specs=(VMEM_SPEC,) * len(out),
        input_output_aliases={6: 0, 7: 1} | ({} if first else {8 + i: 3 + i for i in range(3)}),
        compiler_params=pltpu.CompilerParams(vmem_limit_bytes=STAGE_LIMIT),
        name="backward_stage",
    )(at, *args)
    return result[:2], result[2], result[3:]


def swap_blocks(value, size, swap):
    lane = lax.broadcasted_iota(jnp.int32, value.shape, 1)
    width = value.shape[1]
    swapped = jnp.where(
        lax.rem(lane, 2 * size) < size,
        pltpu.roll(value, width - size, 1),
        pltpu.roll(value, size, 1),
    )
    return jnp.where(swap, swapped, value)


def terms_kernel(at_ref, n_ref, c_ref, g_ref, d_ref, x_ref, own_ref, oth_ref):
    zl, x, c = at_ref[1], at_ref[2], at_ref[3]
    swap = c == 1
    normed = swap_blocks(n_ref[0].astype(F32), 64, swap).astype(BF16)
    ctx = swap_blocks(c_ref[0].astype(F32), 32, swap).astype(BF16)
    scaled = swap_blocks(x_ref[0].astype(F32), 64, swap).astype(BF16)

    def place(value, lo, at_row, rows):
        value = value.astype(BF16)
        count = value.shape[1]
        for pair in range(8):
            rz = lax.rem(pair // 4 + zl, 2)
            rx = lax.rem(pair % 4 - x + 4, 4)
            for which, ref in enumerate((own_ref, oth_ref)):
                at = (2 * pair + which) * rows
                ref[rx, rz, at_row : at_row + rows, lo : lo + count] = value[at : at + rows]

    for col in range(0, 1536, 256):
        place(dot(normed, d_ref[0, :, col : col + 256], 0, 0), col, 0, 64)
    for half in range(2):
        for col in range(0, 512, 256):
            at = half * 512 + col
            place(dot(ctx, g_ref[0, :, at : at + 256], 0, 0), 1536 + col, half * 32, 32)
    place(dot(scaled, jnp.ones((S, 128), BF16), 0, 0), 2048, 0, 64)


def terms(at, rel, normed, ctx, g, d, x):
    def pick(width):
        return pl.BlockSpec((1, S, width), lambda i, at: (lax.rem(at[0] + rel, 4), 0, 0))

    shape = (4, 2, 64, PACK)
    return pl.pallas_call(
        terms_kernel,
        out_shape=(jax.ShapeDtypeStruct(shape, BF16),) * 2,
        grid_spec=pltpu.PrefetchScalarGridSpec(
            num_scalar_prefetch=1,
            grid=(1,),
            in_specs=[pick(D), pick(W), pick(D), pick(3 * W), pick(D)],
            out_specs=[pl.BlockSpec(shape, lambda i, at: (0, 0, 0, 0))] * 2,
        ),
        compiler_params=pltpu.CompilerParams(vmem_limit_bytes=TERMS_LIMIT),
        cost_estimate=pl.CostEstimate(flops=2 * S * D * PACK, bytes_accessed=8 * D * PACK // 2, transcendentals=0),
        name="weight_terms",
    )(at, normed, ctx, g, d, x)


def finish_kernel(own_ref, other_ref, qkv_ref, out_ref, gain_ref):
    total = own_ref[...].astype(F32) + other_ref[...].astype(F32)
    qkv_ref[0] = total[:, :1536]
    out_ref[0, :, :512] = total[:32, 1536:2048]
    out_ref[0, :, 512:] = total[32:, 1536:2048]
    gain_ref[...] = total[:, 2048:].T[:1]


def finish(own, other):
    return pl.pallas_call(
        finish_kernel,
        out_shape=(
            jax.ShapeDtypeStruct((1, 64, 1536), F32),
            jax.ShapeDtypeStruct((1, 32, 1024), F32),
            jax.ShapeDtypeStruct((1, 64), F32),
        ),
        in_specs=[VMEM_SPEC] * 2,
        out_specs=(VMEM_SPEC,) * 3,
        compiler_params=pltpu.CompilerParams(vmem_limit_bytes=STAGE_LIMIT),
        name="finish",
    )(*in_vmem(own, other))


def body(inputs, segment_ids, cotangent, gains, w_qkv, w_out):
    section = lax.axis_index("section")
    replica = lax.axis_index("dp")
    zh, y = section // 4, section % 4
    zl, x, c = replica // 8, (replica // 2) % 4, replica % 2
    at = jnp.stack([y, zl, x, c, zh]).astype(jnp.int32)

    upper = zl == 1
    mine = w_qkv[0], w_out[0]
    theirs = tuple(move(rows, "zl", 1) for rows in mine)

    def by_level(take):
        own_rows, other_rows = take(*mine), take(*theirs)
        return jnp.stack(
            [jnp.where(upper, other_rows, own_rows), jnp.where(upper, own_rows, other_rows)], 0
        )

    a_own = by_level(lambda qkv, out: qkv[:, :1024])
    b_own = by_level(
        lambda qkv, out: jnp.concatenate(
            [qkv[:, 1024:], jnp.concatenate([out[:, :512], out[:, 512:]], 0)], 1
        )
    )
    gain_rows = jnp.broadcast_to(jnp.pad(gains, ((0, 15), (0, 0)))[None], (2, 16, D))
    first = c == 0
    a_near, b_near = gather_rings(
        first, (a_own, "x"), (jnp.concatenate([b_own, gain_rows], 1), "y")
    )
    gain_parts = jnp.stack([block[0, 64] for block in b_near], 0)
    gain = jnp.take(gain_parts, (jnp.arange(4) - y) % 4, axis=0).astype(F32)[:, None]

    start = lax.dynamic_slice_in_dim(inputs, y * S, S, 0)
    target = lax.dynamic_slice_in_dim(cotangent, y * S, S, 0)
    segment = lax.dynamic_index_in_dim(segment_ids, y, 0, keepdims=False)
    position = jnp.arange(S)
    allowed = (position[:, None] <= position[None, :]) & (segment[:, None] == segment[None, :])
    bias = jnp.where(allowed, 0.0, -1e30).astype(F32)
    bias = jnp.concatenate([bias] * 4, 1)

    rows = jnp.stack(a_near, 0), jnp.stack([block[:, :64] for block in b_near], 0)
    rows, at, gain, bias, start, target = lax.optimization_barrier((rows, at, gain, bias, start, target))
    a_all, b_all = gather_rings(first, (rows[0], "y"), (rows[1], "x"))
    own = a_all + b_all
    other = [None if i % 4 == 2 else move(piece, "core", 1) for i, piece in enumerate(own)]
    weights = load_near(at, own + other)
    own[2], own[6], weights = lax.optimization_barrier((own[2], own[6], weights))
    other[2], other[6] = move(own[2], "core", 1), move(own[6], "core", 1)
    pieces = own + other

    saved = kept = None
    hidden, grad = start, target
    for stage in range(4):
        weights, hidden, saved = forward_stage(stage, at, hidden, bias, gain, weights, saved, pieces)
        if stage < 3:
            hidden = move(hidden, "zh", -1, only=stage)
    for stage in reversed(range(4)):
        weights, grad, kept = backward_stage(stage, at, grad, gain, saved, weights, kept)
        if stage > 0:
            grad = move(grad, "zh", 1, only=stage)

    sums = {}
    for rel in (2, 1, 3, 0):
        own_term, other_term = terms(at, rel, saved[1], saved[4], kept[0], kept[1], kept[2])
        sums[rel] = add(own_term, move(other_term, "core", 1))
    a = {rel: sums[rel][..., :HALF] for rel in sums}
    b = {rx: jnp.stack([sums[ry][rx, :, :, HALF:] for ry in range(4)], 0) for rx in range(4)}
    a_y, b_x = scatter_rings(first, (a[2], a[1], a[3], a[0], "y"), (b[2], b[1], b[3], b[0], "x"))
    a_x, b_y = scatter_rings(
        first, (a_y[2], a_y[1], a_y[3], a_y[0], "x"), (b_x[2], b_x[1], b_x[3], b_x[0], "y")
    )
    last = jnp.concatenate([a_x, b_y], -1)
    return finish(last[0], move(last[1], "zl", 1))


def solution(mesh):
    placed = (
        P("dp", None),
        P("dp", None),
        P("dp", None),
        P("section", None),
        P("section", "dp", None),
        P("section", "dp", None),
    )
    return jax.shard_map(
        body,
        mesh=mesh,
        in_specs=placed,
        out_specs=(P("section", "dp", None), P("section", "dp", None), P("section", "dp")),
        check_vma=False,
    )
```

```python
import functools

import jax
import jax.numpy as jnp
from jax import lax
from jax.experimental import pallas as pl
from jax.experimental.pallas import tpu as pltpu
from jax.sharding import PartitionSpec as P

D = 1024
W = 512
S = 64
STAGE = 4
FOUR = 256
PACK = 2176
HALF = 1024
SIZES = {"zh": 4, "y": 4, "zl": 2, "x": 4, "core": 2}
BF16 = jnp.bfloat16
F32 = jnp.float32
STAGE_LIMIT = 8 * 1024 * 1024
TERMS_LIMIT = 24 * 1024 * 1024


def dot(a, b, ca, cb):
    return lax.dot_general(a, b, (((ca,), (cb,)), ((), ())), preferred_element_type=F32)


def coords(index):
    out = {}
    for name in ("core", "x", "zl", "y", "zh"):
        out[name] = index % SIZES[name]
        index //= SIZES[name]
    return out


def linear(at):
    index = 0
    for name in ("zh", "y", "zl", "x", "core"):
        index = index * SIZES[name] + at[name]
    return index


def move(value, axis, step, only=None):
    pairs = []
    for index in range(256):
        at = coords(index)
        if only is not None and at["zh"] != only:
            continue
        target = dict(at)
        far = step[at["core"]] if isinstance(step, tuple) else step
        target[axis] = (at[axis] - far) % SIZES[axis]
        pairs.append((index, linear(target)))
    return lax.ppermute(value, ("section", "dp"), pairs)


def gather_rings(first, *rings):
    near = [(move(own, axis, 1), move(own, axis, -1)) for own, axis in rings]
    near = lax.optimization_barrier(near)
    out = []
    for (own, axis), (plus, minus) in zip(rings, near, strict=True):
        far = move(jnp.where(first, plus, minus), axis, (1, -1))
        out.append([own, plus, far, minus])
    return out


def scatter_rings(first, *rings):
    passing = [move(far, axis, (-1, 1)) for far, _, _, _, axis in rings]
    out = []
    for (_, plus, minus, own, axis), far in zip(rings, passing, strict=True):
        zero = jnp.zeros_like(far)
        behind = move(add(plus, jnp.where(first, far, zero)), axis, -1)
        ahead = move(add(minus, jnp.where(first, zero, far)), axis, 1)
        out.append(add(own, behind, ahead))
    return out


def add(*values):
    return functools.reduce(jnp.add, [value.astype(F32) for value in values]).astype(BF16)


WEIGHT = (STAGE, 2, 4, 2, 64, 1024)
SAVED = ((STAGE, S, D), (STAGE, S, D), (STAGE, S, 3 * W), (STAGE, S, W), (STAGE, S, W))
KEPT = ((STAGE, S, D), (STAGE, S, 3 * W), (STAGE, S, D))
SMEM_SPEC = pl.BlockSpec(memory_space=pltpu.SMEM)
VMEM_SPEC = pl.BlockSpec(memory_space=pltpu.VMEM)
ANY_SPEC = pl.BlockSpec(memory_space=pl.ANY)


def in_vmem(*arrays):
    return tuple(pltpu.with_memory_space_constraint(array, pltpu.VMEM) for array in arrays)


def head_masks(value):
    head = lax.broadcasted_iota(jnp.int32, (S, FOUR), 1) // 64
    return [jnp.where(head == i, value, 0.0).astype(BF16) for i in range(4)]


def spread(value, masks):
    return jnp.concatenate([value * mask for mask in masks], 0)


def collect(product):
    head = lax.broadcasted_iota(jnp.int32, (S, FOUR), 1) // 64
    out = product[3 * S :]
    for i in (2, 1, 0):
        out = jnp.where(head == i, product[i * S : (i + 1) * S], out)
    return out


def statistics(h):
    centre = jnp.mean(h, axis=-1, keepdims=True)
    centred = h - centre
    variance = jnp.mean(centred * centred, axis=-1, keepdims=True)
    rstd = lax.rsqrt(variance + 1e-05)
    return centred * rstd, rstd


def weights_of(wa, wb, layer):
    both = wb[layer].reshape(16, 64, 1024)
    return (
        wa[layer].reshape(D, 2 * W),
        both[:, :, :W].reshape(D, W),
        both[:, :32, W:].reshape(W, W),
        both[:, 32:, W:].reshape(W, W),
    )


def piece_at(pieces, outer, inner):
    return pieces[outer].at[inner]


def load_weights(at, pieces, wa, wb, sem, far):
    y, x, c = at[0], at[2], at[3]

    def one_layer(layer, carry):
        rel = lax.rem(layer - y + 4, 4)
        for ry in range(4):

            @pl.when(rel == ry)
            def _():
                for rc in range(2):
                    core = lax.rem(c + rc, 2)
                    for rx in range(4):
                        column = lax.rem(x + rx, 4)
                        if (ry == 2) == far:
                            a = piece_at(pieces[rc * 8 : rc * 8 + 4], ry, rx)
                            pltpu.make_async_copy(a, wa.at[layer, :, column, core], sem.at[0, layer]).start()
                        if (rx == 2) == far:
                            b = piece_at(pieces[rc * 8 + 4 : rc * 8 + 8], rx, ry)
                            pltpu.make_async_copy(b, wb.at[layer, :, column, core], sem.at[1, layer]).start()

        return carry

    lax.fori_loop(0, STAGE, one_layer, 0)


def wait_weights(at, layer, wa, wb, sem, far):
    @pl.when((lax.rem(layer - at[0] + 4, 4) == 2) == far)
    def _():
        pltpu.make_async_copy(wa.at[layer], wa.at[layer], sem.at[0, layer]).wait()

    some = wb.at[layer, :, pl.ds(0, 1 if far else 3)]
    pltpu.make_async_copy(some, some, sem.at[1, layer]).wait()


def load_kernel(at, *refs):
    pieces, (wa, wb, sem) = refs[:16], refs[16:]
    load_weights(at, pieces, wa, wb, sem, False)
    for layer in range(STAGE):
        wait_weights(at, layer, wa, wb, sem, False)


def load_near(at, pieces):
    near = [pieces[i] if i % 4 != 2 else pieces[i - 1] for i in range(16)]
    near = [pltpu.with_memory_space_constraint(piece, pltpu.HBM) for piece in near]
    return pl.pallas_call(
        load_kernel,
        out_shape=(pltpu.VMEM(WEIGHT, BF16),) * 2,
        in_specs=[SMEM_SPEC] + [ANY_SPEC] * 16,
        out_specs=(VMEM_SPEC,) * 2,
        scratch_shapes=[pltpu.SemaphoreType.DMA((2, STAGE))],
        compiler_params=pltpu.CompilerParams(vmem_limit_bytes=STAGE_LIMIT),
        cost_estimate=pl.CostEstimate(flops=0, bytes_accessed=24 * D * D, transcendentals=0),
        name="load_near",
    )(at, *near)


def forward_kernel(stage, at, h_ref, bias_ref, gain_ref, *refs):
    first = stage == 0
    if first:
        pieces = [refs[2 + i // 4] if i % 4 == 2 else None for i in range(16)]
        wa, wb, h_out, o_h, o_n, o_qkv, o_p, o_c, sem = refs[6:]
        load_weights(at, pieces, wa, wb, sem, True)
    else:
        wa, wb, h_out, o_h, o_n, o_qkv, o_p, o_c = refs[7:]

    @pl.when(at[4] != stage)
    def _():
        h_out[...] = jnp.zeros_like(h_out)
        if first:
            for layer in range(STAGE):
                wait_weights(at, layer, wa, wb, sem, True)

    @pl.when(at[4] == stage)
    def _():
        h_out[...] = h_ref[...]
        bias = bias_ref[...]
        masks = head_masks(0.125)

        def layer_step(layer, carry):
            hidden = h_out[...]
            o_h[layer] = hidden
            h = hidden.astype(F32)
            xhat, _ = statistics(h)
            normed = (xhat * gain_ref[layer]).astype(BF16)
            o_n[layer] = normed
            if first:
                wait_weights(at, layer, wa, wb, sem, True)
            qk = jnp.dot(normed, wa[layer].reshape(D, 2 * W), preferred_element_type=F32).astype(BF16)
            o_qkv[layer, :, : 2 * W] = qk
            _, w_value, out_left, out_right = weights_of(wa, wb, layer)
            value = jnp.dot(normed, w_value, preferred_element_type=F32).astype(BF16)
            o_qkv[layer, :, 2 * W :] = value
            parts = []
            for at_head in range(0, W, FOUR):
                cut = slice(at_head, at_head + FOUR)
                e = jnp.exp(dot(qk[:, W:][:, cut], spread(qk[:, cut], masks), 1, 1) + bias)
                p = (e * (1.0 / jnp.sum(e, axis=0, keepdims=True))).astype(BF16)
                o_p[layer, :, cut] = p
                parts.append(collect(dot(p, value[:, cut], 0, 0)).astype(BF16))
            ctx = jnp.concatenate(parts, 1)
            o_c[layer] = ctx
            left = jnp.dot(ctx, out_left, preferred_element_type=F32)
            right = jnp.dot(ctx, out_right, preferred_element_type=F32)
            h_out[:, :W] = (h[:, :W] + left).astype(BF16)
            h_out[:, W:] = (h[:, W:] + right).astype(BF16)
            return carry

        lax.fori_loop(0, STAGE, layer_step, 0)


def forward_stage(stage, at, h, bias, gain, weights, saved, pieces):
    first = stage == 0
    out = [pltpu.VMEM(WEIGHT, BF16)] * 2 + [pltpu.VMEM((S, D), BF16)]
    out += [pltpu.VMEM(shape, BF16) for shape in SAVED]
    args = [at, *in_vmem(h, bias, gain)]
    specs = [SMEM_SPEC, VMEM_SPEC, VMEM_SPEC, VMEM_SPEC]
    args += list(in_vmem(*weights))
    specs += [VMEM_SPEC] * 2
    if first:
        args += [pieces[i] for i in range(16) if i % 4 == 2]
        specs += [ANY_SPEC] * 4
        aliases, scratch = {4: 0, 5: 1}, [pltpu.SemaphoreType.DMA((2, STAGE))]
    else:
        args += list(in_vmem(*saved))
        specs += [VMEM_SPEC] * 5
        aliases, scratch = {4: 0, 5: 1} | {6 + i: 3 + i for i in range(5)}, []
    result = pl.pallas_call(
        functools.partial(forward_kernel, stage),
        out_shape=tuple(out),
        in_specs=specs,
        out_specs=(VMEM_SPEC,) * len(out),
        input_output_aliases=aliases,
        scratch_shapes=scratch,
        compiler_params=pltpu.CompilerParams(vmem_limit_bytes=STAGE_LIMIT),
        name="forward_stage",
    )(*args)
    return result[:2], result[2], result[3:]


def backward_kernel(stage, at, g_ref, gain_ref, s_h, s_qkv, s_p, *refs):
    wa, wb, g_out, o_g, o_d, o_x = refs[2:] if stage == 3 else refs[5:]

    @pl.when(at[4] != stage)
    def _():
        g_out[...] = jnp.zeros_like(g_out)

    @pl.when(at[4] == stage)
    def _():
        g_out[...] = g_ref[...]
        masks, scaled = head_masks(1.0), head_masks(0.125)

        def layer_step(step, carry):
            layer = STAGE - 1 - step
            g = g_out[...]
            o_g[layer] = g
            w_qk, w_value, out_left, out_right = weights_of(wa, wb, layer)
            dctx = (dot(g[:, :W], out_left, 1, 1) + dot(g[:, W:], out_right, 1, 1)).astype(BF16)
            both = []
            for lo in range(0, W, FOUR):
                d_rows = spread(dctx[:, lo : lo + FOUR], masks)
                p = s_p[layer, :, lo : lo + FOUR]
                pf = p.astype(F32)
                t = pf * dot(s_qkv[layer, :, 2 * W + lo : 2 * W + lo + FOUR], d_rows, 1, 1)
                o_d[layer, :, 2 * W + lo : 2 * W + lo + FOUR] = dot(p, d_rows, 1, 0).astype(BF16)
                both.append((t - pf * jnp.sum(t, axis=0, keepdims=True)).astype(BF16))
            for lo, ds in zip(range(0, W, FOUR), both, strict=True):
                q_rows = spread(s_qkv[layer, :, lo : lo + FOUR], scaled)
                o_d[layer, :, W + lo : W + lo + FOUR] = dot(ds, q_rows, 1, 0).astype(BF16)
            for lo, ds in zip(range(0, W, FOUR), both, strict=True):
                dq = collect(dot(ds, s_qkv[layer, :, W + lo : W + lo + FOUR], 0, 0)) * 0.125
                o_d[layer, :, lo : lo + FOUR] = dq.astype(BF16)
            dn = dot(o_d[layer, :, 2 * W :], w_value, 1, 1) + dot(o_d[layer, :, : 2 * W], w_qk, 1, 1)
            xhat, rstd = statistics(s_h[layer].astype(F32))
            o_x[layer] = (dn * xhat).astype(BF16)
            gd = dn * gain_ref[layer]
            mean_g = jnp.mean(gd, axis=-1, keepdims=True)
            mean_gx = jnp.mean(gd * xhat, axis=-1, keepdims=True)
            g_out[...] = (g.astype(F32) + rstd * (gd - mean_g - xhat * mean_gx)).astype(BF16)
            return carry

        lax.fori_loop(0, STAGE, layer_step, 0)


def backward_stage(stage, at, g, gain, saved, weights, kept):
    first = stage == 3
    args = in_vmem(g, gain, saved[0], saved[2], saved[3], *weights, *(() if first else kept))
    out = (pltpu.VMEM(WEIGHT, BF16),) * 2 + (pltpu.VMEM((S, D), BF16),)
    out += tuple(pltpu.VMEM(shape, BF16) for shape in KEPT)
    result = pl.pallas_call(
        functools.partial(backward_kernel, stage),
        out_shape=out,
        in_specs=[SMEM_SPEC] + [VMEM_SPEC] * len(args),
        out_specs=(VMEM_SPEC,) * len(out),
        input_output_aliases={6: 0, 7: 1} | ({} if first else {8 + i: 3 + i for i in range(3)}),
        compiler_params=pltpu.CompilerParams(vmem_limit_bytes=STAGE_LIMIT),
        name="backward_stage",
    )(at, *args)
    return result[:2], result[2], result[3:]


def swap_blocks(value, size, swap):
    lane = lax.broadcasted_iota(jnp.int32, value.shape, 1)
    width = value.shape[1]
    swapped = jnp.where(
        lax.rem(lane, 2 * size) < size,
        pltpu.roll(value, width - size, 1),
        pltpu.roll(value, size, 1),
    )
    return jnp.where(swap, swapped, value)


def terms_kernel(at_ref, n_ref, c_ref, g_ref, d_ref, x_ref, own_a, own_b, oth_a, oth_b):
    zl, x, c = at_ref[1], at_ref[2], at_ref[3]
    swap = c == 1
    normed = swap_blocks(n_ref[0].astype(F32), 64, swap).astype(BF16)
    ctx = swap_blocks(c_ref[0].astype(F32), 32, swap).astype(BF16)
    scaled = swap_blocks(x_ref[0].astype(F32), 64, swap).astype(BF16)

    def place(value, lo, at_row, rows):
        value = value.astype(BF16)
        count = value.shape[1]
        for pair in range(8):
            rz = lax.rem(pair // 4 + zl, 2)
            rx = lax.rem(pair % 4 - x + 4, 4)
            for which, (ref_a, ref_b) in enumerate(((own_a, own_b), (oth_a, oth_b))):
                at = (2 * pair + which) * rows
                ref, start = (ref_a, lo) if lo < HALF else (ref_b, lo - HALF)
                ref[rx, rz, at_row : at_row + rows, start : start + count] = value[at : at + rows]

    for col in range(0, 1536, 256):
        place(dot(normed, d_ref[0, :, col : col + 256], 0, 0), col, 0, 64)
    for half in range(2):
        for col in range(0, 512, 256):
            at = half * 512 + col
            place(dot(ctx, g_ref[0, :, at : at + 256], 0, 0), 1536 + col, half * 32, 32)
    place(dot(scaled, jnp.ones((S, 128), BF16), 0, 0), 2048, 0, 64)


def terms(at, rel, normed, ctx, g, d, x):
    def pick(width):
        return pl.BlockSpec((1, S, width), lambda i, at: (lax.rem(at[0] + rel, 4), 0, 0))

    shapes = [(4, 2, 64, HALF), (4, 2, 64, PACK - HALF)] * 2
    return pl.pallas_call(
        terms_kernel,
        out_shape=tuple(jax.ShapeDtypeStruct(shape, BF16) for shape in shapes),
        grid_spec=pltpu.PrefetchScalarGridSpec(
            num_scalar_prefetch=1,
            grid=(1,),
            in_specs=[pick(D), pick(W), pick(D), pick(3 * W), pick(D)],
            out_specs=[pl.BlockSpec(shape, lambda i, at: (0, 0, 0, 0)) for shape in shapes],
        ),
        compiler_params=pltpu.CompilerParams(vmem_limit_bytes=TERMS_LIMIT),
        cost_estimate=pl.CostEstimate(flops=2 * S * D * PACK, bytes_accessed=8 * D * PACK // 2, transcendentals=0),
        name="weight_terms",
    )(at, normed, ctx, g, d, x)


def finish_kernel(own_ref, other_ref, qkv_ref, out_ref, gain_ref):
    total = own_ref[...].astype(F32) + other_ref[...].astype(F32)
    qkv_ref[0] = total[:, :1536]
    out_ref[0, :, :512] = total[:32, 1536:2048]
    out_ref[0, :, 512:] = total[32:, 1536:2048]
    gain_ref[...] = total[:, 2048:].T[:1]


def finish(own, other):
    return pl.pallas_call(
        finish_kernel,
        out_shape=(
            jax.ShapeDtypeStruct((1, 64, 1536), F32),
            jax.ShapeDtypeStruct((1, 32, 1024), F32),
            jax.ShapeDtypeStruct((1, 64), F32),
        ),
        in_specs=[VMEM_SPEC] * 2,
        out_specs=(VMEM_SPEC,) * 3,
        compiler_params=pltpu.CompilerParams(vmem_limit_bytes=STAGE_LIMIT),
        name="finish",
    )(*in_vmem(own, other))


def body(inputs, segment_ids, cotangent, gains, w_qkv, w_out):
    section = lax.axis_index("section")
    replica = lax.axis_index("dp")
    zh, y = section // 4, section % 4
    zl, x, c = replica // 8, (replica // 2) % 4, replica % 2
    at = jnp.stack([y, zl, x, c, zh]).astype(jnp.int32)

    upper = zl == 1
    mine = w_qkv[0], w_out[0]
    theirs = tuple(move(rows, "zl", 1) for rows in mine)

    def by_level(take):
        own_rows, other_rows = take(*mine), take(*theirs)
        return jnp.stack(
            [jnp.where(upper, other_rows, own_rows), jnp.where(upper, own_rows, other_rows)], 0
        )

    a_own = by_level(lambda qkv, out: qkv[:, :1024])
    b_own = by_level(
        lambda qkv, out: jnp.concatenate(
            [qkv[:, 1024:], jnp.concatenate([out[:, :512], out[:, 512:]], 0)], 1
        )
    )
    gain_rows = jnp.broadcast_to(jnp.pad(gains, ((0, 15), (0, 0)))[None], (2, 16, D))
    first = c == 0
    a_near, b_near = gather_rings(
        first, (a_own, "x"), (jnp.concatenate([b_own, gain_rows], 1), "y")
    )
    gain_parts = jnp.stack([block[0, 64] for block in b_near], 0)
    gain = jnp.take(gain_parts, (jnp.arange(4) - y) % 4, axis=0).astype(F32)[:, None]

    start = lax.dynamic_slice_in_dim(inputs, y * S, S, 0)
    target = lax.dynamic_slice_in_dim(cotangent, y * S, S, 0)
    segment = lax.dynamic_index_in_dim(segment_ids, y, 0, keepdims=False)
    position = jnp.arange(S)
    allowed = (position[:, None] <= position[None, :]) & (segment[:, None] == segment[None, :])
    bias = jnp.where(allowed, 0.0, -1e30).astype(F32)
    bias = jnp.concatenate([bias] * 4, 1)

    rows = jnp.stack(a_near, 0), jnp.stack([block[:, :64] for block in b_near], 0)
    rows, at, gain, bias, start, target = lax.optimization_barrier((rows, at, gain, bias, start, target))
    a_all, b_all = gather_rings(first, (rows[0], "y"), (rows[1], "x"))
    own = a_all + b_all
    other = [None if i % 4 == 2 else move(piece, "core", 1) for i, piece in enumerate(own)]
    weights = load_near(at, own + other)
    for i in (2, 6):
        own[i], weights = lax.optimization_barrier((own[i], weights))
        other[i] = move(own[i], "core", 1)
    pieces = own + other

    saved = kept = None
    hidden, grad = start, target
    for stage in range(4):
        weights, hidden, saved = forward_stage(stage, at, hidden, bias, gain, weights, saved, pieces)
        if stage < 3:
            hidden = move(hidden, "zh", -1, only=stage)
    for stage in reversed(range(4)):
        weights, grad, kept = backward_stage(stage, at, grad, gain, saved, weights, kept)
        if stage > 0:
            grad = move(grad, "zh", 1, only=stage)

    made = {
        rel: terms(at, rel, saved[1], saved[4], kept[0], kept[1], kept[2]) for rel in (2, 1, 3, 0)
    }
    a = {2: add(made[2][0], move(made[2][2], "core", 1))}
    b_rows = {rel: add(made[rel][1], move(made[rel][3], "core", 1)) for rel in (2, 1, 3, 0)}
    b = {rx: jnp.stack([b_rows[ry][rx] for ry in range(4)], 0) for rx in range(4)}
    rest = {rel: made[rel][2] for rel in (1, 3, 0)}
    rest, b[2] = lax.optimization_barrier((rest, b[2]))
    a |= {rel: add(made[rel][0], move(rest[rel], "core", 1)) for rel in (1, 3, 0)}
    a_y, b_x = scatter_rings(first, (a[2], a[1], a[3], a[0], "y"), (b[2], b[1], b[3], b[0], "x"))
    a_x, b_y = scatter_rings(
        first, (a_y[2], a_y[1], a_y[3], a_y[0], "x"), (b_x[2], b_x[1], b_x[3], b_x[0], "y")
    )
    last = jnp.concatenate([a_x, b_y], -1)
    return finish(last[0], move(last[1], "zl", 1))


def solution(mesh):
    placed = (
        P("dp", None),
        P("dp", None),
        P("dp", None),
        P("section", None),
        P("section", "dp", None),
        P("section", "dp", None),
    )
    return jax.shard_map(
        body,
        mesh=mesh,
        in_specs=placed,
        out_specs=(P("section", "dp", None), P("section", "dp", None), P("section", "dp")),
        check_vma=False,
    )
```

```python
import functools

import jax
import jax.numpy as jnp
from jax import lax
from jax.experimental import pallas as pl
from jax.experimental.pallas import tpu as pltpu
from jax.sharding import PartitionSpec as P

D = 1024
W = 512
S = 64
STAGE = 4
FOUR = 256
PACK = 2176
HALF = 1152
SIZES = {"zh": 4, "y": 4, "zl": 2, "x": 4, "core": 2}
BF16 = jnp.bfloat16
F32 = jnp.float32
STAGE_LIMIT = 8 * 1024 * 1024
TERMS_LIMIT = 24 * 1024 * 1024


def dot(a, b, ca, cb):
    return lax.dot_general(a, b, (((ca,), (cb,)), ((), ())), preferred_element_type=F32)


def coords(index):
    out = {}
    for name in ("core", "x", "zl", "y", "zh"):
        out[name] = index % SIZES[name]
        index //= SIZES[name]
    return out


def linear(at):
    index = 0
    for name in ("zh", "y", "zl", "x", "core"):
        index = index * SIZES[name] + at[name]
    return index


def move(value, axis, step, only=None):
    pairs = []
    for index in range(256):
        at = coords(index)
        if only is not None and at["zh"] != only:
            continue
        target = dict(at)
        far = step[at["core"]] if isinstance(step, tuple) else step
        target[axis] = (at[axis] - far) % SIZES[axis]
        pairs.append((index, linear(target)))
    return lax.ppermute(value, ("section", "dp"), pairs)


def gather_rings(first, *rings):
    near = [(move(own, axis, 1), move(own, axis, -1)) for own, axis in rings]
    near = lax.optimization_barrier(near)
    out = []
    for (own, axis), (plus, minus) in zip(rings, near, strict=True):
        far = move(jnp.where(first, plus, minus), axis, (1, -1))
        out.append([own, plus, far, minus])
    return out


def scatter_rings(first, *rings):
    passing = [move(far, axis, (-1, 1)) for far, _, _, _, axis in rings]
    out = []
    for (_, plus, minus, own, axis), far in zip(rings, passing, strict=True):
        zero = jnp.zeros_like(far)
        behind = move(add(plus, jnp.where(first, far, zero)), axis, -1)
        ahead = move(add(minus, jnp.where(first, zero, far)), axis, 1)
        out.append(add(own, behind, ahead))
    return out


def add(*values):
    return functools.reduce(jnp.add, [value.astype(F32) for value in values]).astype(BF16)


WEIGHT = (STAGE, 2, 4, 2, 64, 1024)
SAVED = ((STAGE, S, D), (STAGE, S, D), (STAGE, S, 3 * W), (STAGE, S, W), (STAGE, S, W))
KEPT = ((STAGE, S, D), (STAGE, S, 3 * W), (STAGE, S, D))
SMEM_SPEC = pl.BlockSpec(memory_space=pltpu.SMEM)
VMEM_SPEC = pl.BlockSpec(memory_space=pltpu.VMEM)
ANY_SPEC = pl.BlockSpec(memory_space=pl.ANY)


def in_vmem(*arrays):
    return tuple(pltpu.with_memory_space_constraint(array, pltpu.VMEM) for array in arrays)


def head_masks(value):
    head = lax.broadcasted_iota(jnp.int32, (S, FOUR), 1) // 64
    return [jnp.where(head == i, value, 0.0).astype(BF16) for i in range(4)]


def spread(value, masks):
    return jnp.concatenate([value * mask for mask in masks], 0)


def collect(product):
    head = lax.broadcasted_iota(jnp.int32, (S, FOUR), 1) // 64
    out = product[3 * S :]
    for i in (2, 1, 0):
        out = jnp.where(head == i, product[i * S : (i + 1) * S], out)
    return out


def statistics(h):
    centre = jnp.mean(h, axis=-1, keepdims=True)
    centred = h - centre
    variance = jnp.mean(centred * centred, axis=-1, keepdims=True)
    rstd = lax.rsqrt(variance + 1e-05)
    return centred * rstd, rstd


def weights_of(wa, wb, layer):
    both = wb[layer].reshape(16, 64, 1024)
    return (
        wa[layer].reshape(D, 2 * W),
        both[:, :, :W].reshape(D, W),
        both[:, :32, W:].reshape(W, W),
        both[:, 32:, W:].reshape(W, W),
    )


def piece_at(pieces, outer, inner):
    return pieces[outer].at[inner]


def load_weights(at, pieces, wa, wb, sem, far):
    y, x, c = at[0], at[2], at[3]

    def one_layer(layer, carry):
        rel = lax.rem(layer - y + 4, 4)
        for ry in range(4):

            @pl.when(rel == ry)
            def _():
                for rc in range(2):
                    core = lax.rem(c + rc, 2)
                    for rx in range(4):
                        column = lax.rem(x + rx, 4)
                        if (ry == 2) == far:
                            a = piece_at(pieces[rc * 8 : rc * 8 + 4], ry, rx)
                            pltpu.make_async_copy(a, wa.at[layer, :, column, core], sem.at[0, layer]).start()
                        if (rx == 2) == far:
                            b = piece_at(pieces[rc * 8 + 4 : rc * 8 + 8], rx, ry)
                            pltpu.make_async_copy(b, wb.at[layer, :, column, core], sem.at[1, layer]).start()

        return carry

    lax.fori_loop(0, STAGE, one_layer, 0)


def wait_weights(at, layer, wa, wb, sem, far):
    @pl.when((lax.rem(layer - at[0] + 4, 4) == 2) == far)
    def _():
        pltpu.make_async_copy(wa.at[layer], wa.at[layer], sem.at[0, layer]).wait()

    some = wb.at[layer, :, pl.ds(0, 1 if far else 3)]
    pltpu.make_async_copy(some, some, sem.at[1, layer]).wait()


def load_kernel(at, *refs):
    pieces, (wa, wb, sem) = refs[:16], refs[16:]
    load_weights(at, pieces, wa, wb, sem, False)
    for layer in range(STAGE):
        wait_weights(at, layer, wa, wb, sem, False)


def load_near(at, pieces):
    near = [pieces[i] if i % 4 != 2 else pieces[i - 1] for i in range(16)]
    near = [pltpu.with_memory_space_constraint(piece, pltpu.HBM) for piece in near]
    return pl.pallas_call(
        load_kernel,
        out_shape=(pltpu.VMEM(WEIGHT, BF16),) * 2,
        in_specs=[SMEM_SPEC] + [ANY_SPEC] * 16,
        out_specs=(VMEM_SPEC,) * 2,
        scratch_shapes=[pltpu.SemaphoreType.DMA((2, STAGE))],
        compiler_params=pltpu.CompilerParams(vmem_limit_bytes=STAGE_LIMIT),
        cost_estimate=pl.CostEstimate(flops=0, bytes_accessed=24 * D * D, transcendentals=0),
        name="load_near",
    )(at, *near)


def forward_kernel(stage, at, h_ref, bias_ref, gain_ref, *refs):
    first = stage == 0
    if first:
        pieces = [refs[2 + i // 4] if i % 4 == 2 else None for i in range(16)]
        wa, wb, h_out, o_h, o_n, o_qkv, o_p, o_c, sem = refs[6:]
        load_weights(at, pieces, wa, wb, sem, True)
    else:
        wa, wb, h_out, o_h, o_n, o_qkv, o_p, o_c = refs[7:]

    @pl.when(at[4] != stage)
    def _():
        h_out[...] = jnp.zeros_like(h_out)
        if first:
            for layer in range(STAGE):
                wait_weights(at, layer, wa, wb, sem, True)

    @pl.when(at[4] == stage)
    def _():
        h_out[...] = h_ref[...]
        bias = bias_ref[...]
        masks = head_masks(0.125)

        def layer_step(layer, carry):
            hidden = h_out[...]
            o_h[layer] = hidden
            h = hidden.astype(F32)
            xhat, _ = statistics(h)
            normed = (xhat * gain_ref[layer]).astype(BF16)
            o_n[layer] = normed
            if first:
                wait_weights(at, layer, wa, wb, sem, True)
            qk = jnp.dot(normed, wa[layer].reshape(D, 2 * W), preferred_element_type=F32).astype(BF16)
            o_qkv[layer, :, : 2 * W] = qk
            _, w_value, out_left, out_right = weights_of(wa, wb, layer)
            value = jnp.dot(normed, w_value, preferred_element_type=F32).astype(BF16)
            o_qkv[layer, :, 2 * W :] = value
            parts = []
            for at_head in range(0, W, FOUR):
                cut = slice(at_head, at_head + FOUR)
                e = jnp.exp(dot(qk[:, W:][:, cut], spread(qk[:, cut], masks), 1, 1) + bias)
                p = (e * (1.0 / jnp.sum(e, axis=0, keepdims=True))).astype(BF16)
                o_p[layer, :, cut] = p
                parts.append(collect(dot(p, value[:, cut], 0, 0)).astype(BF16))
            ctx = jnp.concatenate(parts, 1)
            o_c[layer] = ctx
            left = jnp.dot(ctx, out_left, preferred_element_type=F32)
            right = jnp.dot(ctx, out_right, preferred_element_type=F32)
            h_out[:, :W] = (h[:, :W] + left).astype(BF16)
            h_out[:, W:] = (h[:, W:] + right).astype(BF16)
            return carry

        lax.fori_loop(0, STAGE, layer_step, 0)


def forward_stage(stage, at, h, bias, gain, weights, saved, pieces):
    first = stage == 0
    out = [pltpu.VMEM(WEIGHT, BF16)] * 2 + [pltpu.VMEM((S, D), BF16)]
    out += [pltpu.VMEM(shape, BF16) for shape in SAVED]
    args = [at, *in_vmem(h, bias, gain)]
    specs = [SMEM_SPEC, VMEM_SPEC, VMEM_SPEC, VMEM_SPEC]
    args += list(in_vmem(*weights))
    specs += [VMEM_SPEC] * 2
    if first:
        args += [pieces[i] for i in range(16) if i % 4 == 2]
        specs += [ANY_SPEC] * 4
        aliases, scratch = {4: 0, 5: 1}, [pltpu.SemaphoreType.DMA((2, STAGE))]
    else:
        args += list(in_vmem(*saved))
        specs += [VMEM_SPEC] * 5
        aliases, scratch = {4: 0, 5: 1} | {6 + i: 3 + i for i in range(5)}, []
    result = pl.pallas_call(
        functools.partial(forward_kernel, stage),
        out_shape=tuple(out),
        in_specs=specs,
        out_specs=(VMEM_SPEC,) * len(out),
        input_output_aliases=aliases,
        scratch_shapes=scratch,
        compiler_params=pltpu.CompilerParams(vmem_limit_bytes=STAGE_LIMIT),
        name="forward_stage",
    )(*args)
    return result[:2], result[2], result[3:]


def backward_kernel(stage, at, g_ref, gain_ref, s_h, s_qkv, s_p, *refs):
    wa, wb, g_out, o_g, o_d, o_x = refs[2:] if stage == 3 else refs[5:]

    @pl.when(at[4] != stage)
    def _():
        g_out[...] = jnp.zeros_like(g_out)

    @pl.when(at[4] == stage)
    def _():
        g_out[...] = g_ref[...]
        masks, scaled = head_masks(1.0), head_masks(0.125)

        def layer_step(step, carry):
            layer = STAGE - 1 - step
            g = g_out[...]
            o_g[layer] = g
            w_qk, w_value, out_left, out_right = weights_of(wa, wb, layer)
            dctx = (dot(g[:, :W], out_left, 1, 1) + dot(g[:, W:], out_right, 1, 1)).astype(BF16)
            both = []
            for lo in range(0, W, FOUR):
                d_rows = spread(dctx[:, lo : lo + FOUR], masks)
                p = s_p[layer, :, lo : lo + FOUR]
                pf = p.astype(F32)
                t = pf * dot(s_qkv[layer, :, 2 * W + lo : 2 * W + lo + FOUR], d_rows, 1, 1)
                o_d[layer, :, 2 * W + lo : 2 * W + lo + FOUR] = dot(p, d_rows, 1, 0).astype(BF16)
                both.append((t - pf * jnp.sum(t, axis=0, keepdims=True)).astype(BF16))
            for lo, ds in zip(range(0, W, FOUR), both, strict=True):
                q_rows = spread(s_qkv[layer, :, lo : lo + FOUR], scaled)
                o_d[layer, :, W + lo : W + lo + FOUR] = dot(ds, q_rows, 1, 0).astype(BF16)
            for lo, ds in zip(range(0, W, FOUR), both, strict=True):
                dq = collect(dot(ds, s_qkv[layer, :, W + lo : W + lo + FOUR], 0, 0)) * 0.125
                o_d[layer, :, lo : lo + FOUR] = dq.astype(BF16)
            dn = dot(o_d[layer, :, 2 * W :], w_value, 1, 1) + dot(o_d[layer, :, : 2 * W], w_qk, 1, 1)
            xhat, rstd = statistics(s_h[layer].astype(F32))
            o_x[layer] = (dn * xhat).astype(BF16)
            gd = dn * gain_ref[layer]
            mean_g = jnp.mean(gd, axis=-1, keepdims=True)
            mean_gx = jnp.mean(gd * xhat, axis=-1, keepdims=True)
            g_out[...] = (g.astype(F32) + rstd * (gd - mean_g - xhat * mean_gx)).astype(BF16)
            return carry

        lax.fori_loop(0, STAGE, layer_step, 0)


def backward_stage(stage, at, g, gain, saved, weights, kept):
    first = stage == 3
    args = in_vmem(g, gain, saved[0], saved[2], saved[3], *weights, *(() if first else kept))
    out = (pltpu.VMEM(WEIGHT, BF16),) * 2 + (pltpu.VMEM((S, D), BF16),)
    out += tuple(pltpu.VMEM(shape, BF16) for shape in KEPT)
    result = pl.pallas_call(
        functools.partial(backward_kernel, stage),
        out_shape=out,
        in_specs=[SMEM_SPEC] + [VMEM_SPEC] * len(args),
        out_specs=(VMEM_SPEC,) * len(out),
        input_output_aliases={6: 0, 7: 1} | ({} if first else {8 + i: 3 + i for i in range(3)}),
        compiler_params=pltpu.CompilerParams(vmem_limit_bytes=STAGE_LIMIT),
        name="backward_stage",
    )(at, *args)
    return result[:2], result[2], result[3:]


def swap_blocks(value, size, swap):
    lane = lax.broadcasted_iota(jnp.int32, value.shape, 1)
    width = value.shape[1]
    swapped = jnp.where(
        lax.rem(lane, 2 * size) < size,
        pltpu.roll(value, width - size, 1),
        pltpu.roll(value, size, 1),
    )
    return jnp.where(swap, swapped, value)


def terms_kernel(at_ref, n_ref, c_ref, g_ref, d_ref, x_ref, own_a, own_b, oth_a, oth_b):
    zl, x, c = at_ref[1], at_ref[2], at_ref[3]
    swap = c == 1
    normed = swap_blocks(n_ref[0].astype(F32), 64, swap).astype(BF16)
    ctx = swap_blocks(c_ref[0].astype(F32), 32, swap).astype(BF16)
    scaled = swap_blocks(x_ref[0].astype(F32), 64, swap).astype(BF16)

    def place(value, lo, at_row, rows):
        value = value.astype(BF16)
        count = value.shape[1]
        for pair in range(8):
            rz = lax.rem(pair // 4 + zl, 2)
            rx = lax.rem(pair % 4 - x + 4, 4)
            for which, (ref_a, ref_b) in enumerate(((own_a, own_b), (oth_a, oth_b))):
                at = (2 * pair + which) * rows
                ref, start = (ref_a, lo) if lo < HALF else (ref_b, lo - HALF)
                ref[rx, rz, at_row : at_row + rows, start : start + count] = value[at : at + rows]

    for col, count in [(0, 256), (256, 256), (512, 256), (768, 256), (1024, 128), (1152, 128), (1280, 256)]:
        place(dot(normed, d_ref[0, :, col : col + count], 0, 0), col, 0, 64)
    for half in range(2):
        for col in range(0, 512, 256):
            at = half * 512 + col
            place(dot(ctx, g_ref[0, :, at : at + 256], 0, 0), 1536 + col, half * 32, 32)
    place(dot(scaled, jnp.ones((S, 128), BF16), 0, 0), 2048, 0, 64)


def terms(at, rel, normed, ctx, g, d, x):
    def pick(width):
        return pl.BlockSpec((1, S, width), lambda i, at: (lax.rem(at[0] + rel, 4), 0, 0))

    shapes = [(4, 2, 64, HALF), (4, 2, 64, PACK - HALF)] * 2
    return pl.pallas_call(
        terms_kernel,
        out_shape=tuple(jax.ShapeDtypeStruct(shape, BF16) for shape in shapes),
        grid_spec=pltpu.PrefetchScalarGridSpec(
            num_scalar_prefetch=1,
            grid=(1,),
            in_specs=[pick(D), pick(W), pick(D), pick(3 * W), pick(D)],
            out_specs=[pl.BlockSpec(shape, lambda i, at: (0, 0, 0, 0)) for shape in shapes],
        ),
        compiler_params=pltpu.CompilerParams(vmem_limit_bytes=TERMS_LIMIT),
        cost_estimate=pl.CostEstimate(flops=2 * S * D * PACK, bytes_accessed=8 * D * PACK // 2, transcendentals=0),
        name="weight_terms",
    )(at, normed, ctx, g, d, x)


def finish_kernel(own_ref, other_ref, qkv_ref, out_ref, gain_ref):
    total = own_ref[...].astype(F32) + other_ref[...].astype(F32)
    qkv_ref[0] = total[:, :1536]
    out_ref[0, :, :512] = total[:32, 1536:2048]
    out_ref[0, :, 512:] = total[32:, 1536:2048]
    gain_ref[...] = total[:, 2048:].T[:1]


def finish(own, other):
    return pl.pallas_call(
        finish_kernel,
        out_shape=(
            jax.ShapeDtypeStruct((1, 64, 1536), F32),
            jax.ShapeDtypeStruct((1, 32, 1024), F32),
            jax.ShapeDtypeStruct((1, 64), F32),
        ),
        in_specs=[VMEM_SPEC] * 2,
        out_specs=(VMEM_SPEC,) * 3,
        compiler_params=pltpu.CompilerParams(vmem_limit_bytes=STAGE_LIMIT),
        name="finish",
    )(*in_vmem(own, other))


def body(inputs, segment_ids, cotangent, gains, w_qkv, w_out):
    section = lax.axis_index("section")
    replica = lax.axis_index("dp")
    zh, y = section // 4, section % 4
    zl, x, c = replica // 8, (replica // 2) % 4, replica % 2
    at = jnp.stack([y, zl, x, c, zh]).astype(jnp.int32)

    upper = zl == 1
    mine = w_qkv[0], w_out[0]
    theirs = tuple(move(rows, "zl", 1) for rows in mine)

    def by_level(take):
        own_rows, other_rows = take(*mine), take(*theirs)
        return jnp.stack(
            [jnp.where(upper, other_rows, own_rows), jnp.where(upper, own_rows, other_rows)], 0
        )

    a_own = by_level(lambda qkv, out: qkv[:, :1024])
    b_own = by_level(
        lambda qkv, out: jnp.concatenate(
            [qkv[:, 1024:], jnp.concatenate([out[:, :512], out[:, 512:]], 0)], 1
        )
    )
    gain_rows = jnp.broadcast_to(jnp.pad(gains, ((0, 15), (0, 0)))[None], (2, 16, D))
    first = c == 0
    a_near, b_near = gather_rings(
        first, (a_own, "x"), (jnp.concatenate([b_own, gain_rows], 1), "y")
    )
    gain_parts = jnp.stack([block[0, 64] for block in b_near], 0)
    gain = jnp.take(gain_parts, (jnp.arange(4) - y) % 4, axis=0).astype(F32)[:, None]

    start = lax.dynamic_slice_in_dim(inputs, y * S, S, 0)
    target = lax.dynamic_slice_in_dim(cotangent, y * S, S, 0)
    segment = lax.dynamic_index_in_dim(segment_ids, y, 0, keepdims=False)
    position = jnp.arange(S)
    allowed = (position[:, None] <= position[None, :]) & (segment[:, None] == segment[None, :])
    bias = jnp.where(allowed, 0.0, -1e30).astype(F32)
    bias = jnp.concatenate([bias] * 4, 1)

    rows = jnp.stack(a_near, 0), jnp.stack([block[:, :64] for block in b_near], 0)
    rows, at, gain, bias, start, target = lax.optimization_barrier((rows, at, gain, bias, start, target))
    a_all, b_all = gather_rings(first, (rows[0], "y"), (rows[1], "x"))
    own = a_all + b_all
    other = [None if i % 4 == 2 else move(piece, "core", 1) for i, piece in enumerate(own)]
    weights = load_near(at, own + other)
    for i in (2, 6):
        own[i], weights = lax.optimization_barrier((own[i], weights))
        other[i] = move(own[i], "core", 1)
    pieces = own + other

    saved = kept = None
    hidden, grad = start, target
    for stage in range(4):
        weights, hidden, saved = forward_stage(stage, at, hidden, bias, gain, weights, saved, pieces)
        if stage < 3:
            hidden = move(hidden, "zh", -1, only=stage)
    for stage in reversed(range(4)):
        weights, grad, kept = backward_stage(stage, at, grad, gain, saved, weights, kept)
        if stage > 0:
            grad = move(grad, "zh", 1, only=stage)

    made = {
        rel: terms(at, rel, saved[1], saved[4], kept[0], kept[1], kept[2]) for rel in (2, 1, 3, 0)
    }
    a = {2: add(made[2][0], move(made[2][2], "core", 1))}
    b_rows = {rel: add(made[rel][1], move(made[rel][3], "core", 1)) for rel in (2, 1, 3, 0)}
    b = {rx: jnp.stack([b_rows[ry][rx] for ry in range(4)], 0) for rx in range(4)}
    rest = {rel: made[rel][2] for rel in (1, 3, 0)}
    rest, b[2] = lax.optimization_barrier((rest, b[2]))
    a |= {rel: add(made[rel][0], move(rest[rel], "core", 1)) for rel in (1, 3, 0)}
    a_y, b_x = scatter_rings(first, (a[2], a[1], a[3], a[0], "y"), (b[2], b[1], b[3], b[0], "x"))
    a_x, b_y = scatter_rings(
        first, (a_y[2], a_y[1], a_y[3], a_y[0], "x"), (b_x[2], b_x[1], b_x[3], b_x[0], "y")
    )
    last = jnp.concatenate([a_x, b_y], -1)
    return finish(last[0], move(last[1], "zl", 1))


def solution(mesh):
    placed = (
        P("dp", None),
        P("dp", None),
        P("dp", None),
        P("section", None),
        P("section", "dp", None),
        P("section", "dp", None),
    )
    return jax.shard_map(
        body,
        mesh=mesh,
        in_specs=placed,
        out_specs=(P("section", "dp", None), P("section", "dp", None), P("section", "dp")),
        check_vma=False,
    )
```
